32 devices in a mesh: dp: 16 (over z, x, core), tensor: 2 (over y).
Axes of the slice: x: 2, y: 2, z: 4, core: 2. Of those that a mesh axis runs over, the one named last changes fastest.
Arguments:
- tokens_in: float32 [40960, 1024], P(('dp', 'tensor')), may hold values from -6 to 6
- condition: bfloat16 [40, 1024], P(None, 'dp'), may hold values from -6 to 6
- out_grad: float32 [40960, 1024], P(('dp', 'tensor')), may hold values from -6 to 6
- qkv_weight: float32 [1024, 3, 1024], P('dp', None, 'tensor'), may hold values from -0.1875 to 0.1875
- out_weight: float32 [1024, 1024], P('tensor', 'dp'), may hold values from -0.375 to 0.375
- up_weight: float32 [1024, 4096], P('dp', 'tensor'), may hold values from -0.1875 to 0.1875
- down_weight: float32 [4096, 1024], P('tensor', 'dp'), may hold values from -0.09375 to 0.09375
- ada_weight: float32 [1024, 6144], P('dp'), may hold values from -0.1875 to 0.1875
- bias_all: float32 [14336], replicated, may hold values from -1.5 to 1.5
- qkv_first: float32 [1024, 3, 1024], P('dp', None, 'tensor'), may hold values from -178.09947 to 178.09947
- out_first: float32 [1024, 1024], P('tensor', 'dp'), may hold values from -32.10734 to 32.10734
- up_first: float32 [1024, 4096], P('dp', 'tensor'), may hold values from -28.16 to 28.16
- down_first: float32 [4096, 1024], P('tensor', 'dp'), may hold values from -56.32 to 56.32
- ada_first: float32 [1024, 6144], P('dp'), may hold values from -53.429844 to 53.429844
- bias_first: float32 [14336], replicated, may hold values from -89.049736 to 89.049736
- qkv_second: float32 [1024, 3, 1024], P('dp', None, 'tensor'), may hold values from 8617.984 to 34406.4
- out_second: float32 [1024, 1024], P('tensor', 'dp'), may hold values from 280.08447 to 1118.208
- up_second: float32 [1024, 4096], P('dp', 'tensor'), may hold values from 215.4496 to 860.16
- down_second: float32 [4096, 1024], P('tensor', 'dp'), may hold values from 861.7984 to 3440.64
- ada_second: float32 [1024, 6144], P('dp'), may hold values from 775.6185 to 3096.576
- bias_second: float32 [14336], replicated, may hold values from 2154.496 to 8601.6
Outputs:
- block_out: float32 [40960, 1024], P(('dp', 'tensor'))
- tokens_grad: float32 [40960, 1024], P(('dp', 'tensor'))
- condition_grad: float32 [40, 1024], P(None, 'dp')
- qkv_first_new: float32 [1024, 3, 1024], P('dp', None, 'tensor')
- qkv_second_new: float32 [1024, 3, 1024], P('dp', None, 'tensor')
- qkv_weight_new: float32 [1024, 3, 1024], P('dp', None, 'tensor')
- out_first_new: float32 [1024, 1024], P('tensor', 'dp')
- out_second_new: float32 [1024, 1024], P('tensor', 'dp')
- out_weight_new: float32 [1024, 1024], P('tensor', 'dp')
- up_first_new: float32 [1024, 4096], P('dp', 'tensor')
- up_second_new: float32 [1024, 4096], P('dp', 'tensor')
- up_weight_new: float32 [1024, 4096], P('dp', 'tensor')
- down_first_new: float32 [4096, 1024], P('tensor', 'dp')
- down_second_new: float32 [4096, 1024], P('tensor', 'dp')
- down_weight_new: float32 [4096, 1024], P('tensor', 'dp')
- ada_first_new: float32 [1024, 6144], P('dp')
- ada_second_new: float32 [1024, 6144], P('dp')
- ada_weight_new: float32 [1024, 6144], P('dp')
- bias_first_new: float32 [14336], replicated
- bias_second_new: float32 [14336], replicated
- bias_all_new: float32 [14336], replicated
The draws below stay inside these ranges and needn't reach their ends.
All inputs are finite; a program needn't handle non-finite values.
Results may differ from the reference program's by a relative error of at most 0.023.
The reference program's roundings to bfloat16 on the way count: a program that leaves them out, or rounds other values in their place, can miss the bound.
Values may be sent and summed in bfloat16 or wider, within the bound.
No kernel may reach another device: no remote copies, remote signals or barrier semaphores. Data moves between devices by JAX's collectives and lax.ppermute only.
A program may use at most 320 MiB of HBM per device.

```python
import math
import jax
import jax.numpy as jnp
from jax import lax

D = 1024
H = 16
HD = 64
FF = 4096
L = 1024
STEP = 10
TOKENS = 40960
NLAT = 40
BIAS = 14336


def shard_levels(stream_key, dims, shards, smallest, top_value):
    level, own = 1.0, jax.random.fold_in(stream_key, 6)
    for dim, shards_of in shards:
        draws = jnp.exp(jax.random.uniform(jax.random.fold_in(own, dim), (shards_of,), jnp.float32, smallest / len(shards), top_value / len(shards)))
        level = level * jnp.repeat(draws, dims[dim] // shards_of).reshape([-1 if axis == dim else 1 for axis in range(len(dims))])
    return level


def noise(key, extent, deviation, bound, shards=(), kind=jnp.bfloat16):
    factor_of = shard_levels(key, extent, shards, -0.22, 0.18) if shards else 1.0
    entries = jax.random.normal(key, extent, jnp.float32) * deviation * factor_of
    return jnp.minimum(jnp.maximum(entries, -bound), bound).astype(kind)


def setup_inputs(seed: int = 0) -> dict:
    key_of = jax.random.split(jax.random.key(seed), 22)
    tokens_in = noise(key_of[0], (TOKENS, D), 1.0, 6.0, ((0, 32),), jnp.float32)
    condition = noise(key_of[1], (NLAT, D), 1.0, 6.0, ((1, 16),))
    out_grad = noise(key_of[2], (TOKENS, D), 1.0, 6.0, ((0, 32),), jnp.float32)
    qkv_weight = noise(key_of[3], (D, 3, D), D ** -0.5, 0.1875, ((0, 16), (2, 2)), jnp.float32)
    out_weight = noise(key_of[4], (D, D), (D // 4) ** -0.5, 0.375, ((0, 2), (1, 16)), jnp.float32)
    up_weight = noise(key_of[5], (D, FF), D ** -0.5, 0.1875, ((0, 16), (1, 2)), jnp.float32)
    down_weight = noise(key_of[6], (FF, D), FF ** -0.5, 0.09375, ((0, 2), (1, 16)), jnp.float32)
    ada_weight = noise(key_of[7], (D, 6 * D), D ** -0.5, 0.1875, ((0, 16),), jnp.float32)
    bias_all = noise(key_of[8], (BIAS,), 0.3, 1.5, (), jnp.float32)
    qkv_first = noise(key_of[9], (D, 3, D), (0.11 * (4.0 * TOKENS) ** 0.5), 178.09947, ((0, 16), (2, 2)), jnp.float32)
    out_first = noise(key_of[10], (D, D), (0.11 * (0.13 * TOKENS) ** 0.5), 32.10734, ((0, 2), (1, 16)), jnp.float32)
    up_first = noise(key_of[11], (D, FF), (0.11 * (0.1 * TOKENS) ** 0.5), 28.16, ((0, 16), (1, 2)), jnp.float32)
    down_first = noise(key_of[12], (FF, D), (0.11 * (0.4 * TOKENS) ** 0.5), 56.32, ((0, 2), (1, 16)), jnp.float32)
    ada_first = noise(key_of[13], (D, 6 * D), (0.11 * (0.36 * TOKENS) ** 0.5), 53.429844, ((0, 16),), jnp.float32)
    bias_first = noise(key_of[14], (BIAS,), (0.11 * (1.0 * TOKENS) ** 0.5), 89.049736, (), jnp.float32)
    qkv_second = jnp.clip(jnp.exp(math.log(34406.4) - 1.3843913 * jax.random.uniform(key_of[15], (D, 3, D), jnp.float32) ** shard_levels(key_of[15], (D, 3, D), ((0, 16), (2, 2)), -0.2, 0.2)), 8617.984, 34406.4)
    out_second = jnp.clip(jnp.exp(math.log(1118.208) - 1.3843914 * jax.random.uniform(key_of[16], (D, D), jnp.float32) ** shard_levels(key_of[16], (D, D), ((0, 2), (1, 16)), -0.2, 0.2)), 280.08447, 1118.208)
    up_second = jnp.clip(jnp.exp(math.log(860.16) - 1.3843914 * jax.random.uniform(key_of[17], (D, FF), jnp.float32) ** shard_levels(key_of[17], (D, FF), ((0, 16), (1, 2)), -0.2, 0.2)), 215.4496, 860.16)
    down_second = jnp.clip(jnp.exp(math.log(3440.64) - 1.3843914 * jax.random.uniform(key_of[18], (FF, D), jnp.float32) ** shard_levels(key_of[18], (FF, D), ((0, 2), (1, 16)), -0.2, 0.2)), 861.7984, 3440.64)
    ada_second = jnp.clip(jnp.exp(math.log(3096.576) - 1.3843914 * jax.random.uniform(key_of[19], (D, 6 * D), jnp.float32) ** shard_levels(key_of[19], (D, 6 * D), ((0, 16),), -0.2, 0.2)), 775.6185, 3096.576)
    bias_second = jnp.clip(jnp.exp(jax.random.uniform(key_of[20], (BIAS,), jnp.float32, math.log(2154.496), math.log(8601.6))), 2154.496, 8601.6)
    return {"tokens_in": tokens_in, "condition": condition, "out_grad": out_grad, "qkv_weight": qkv_weight, "out_weight": out_weight, "up_weight": up_weight, "down_weight": down_weight, "ada_weight": ada_weight, "bias_all": bias_all, "qkv_first": qkv_first, "out_first": out_first, "up_first": up_first, "down_first": down_first, "ada_first": ada_first, "bias_first": bias_first, "qkv_second": qkv_second, "out_second": out_second, "up_second": up_second, "down_second": down_second, "ada_second": ada_second, "bias_second": bias_second}


@jax.custom_vjp
def low(v):
    return lax.optimization_barrier(v.astype(jnp.bfloat16)).astype(jnp.float32)

@jax.custom_vjp
def low_back(v):
    return v

def low_keep(v):
    return (low(v), None)

def low_pass(kept, grad):
    return (grad,)

def back_keep(v):
    return (v, None)

def back_low(kept, grad):
    return (low(grad),)
low.defvjp(low_keep, low_pass)
low_back.defvjp(back_keep, back_low)
eps_norm = 1e-06
beta_one = 0.9
beta_two = 0.95
adam_eps = 1e-08
decay_rate = 0.01
highest = lax.Precision.HIGHEST

def matmul(left_side, right_side):
    return jnp.dot(left_side, right_side, precision=highest, preferred_element_type=jnp.float32)

def layer_norm(values):
    center = values - lax.optimization_barrier(jnp.mean(values, axis=-1, keepdims=True))
    spread = lax.optimization_barrier(jnp.mean(center * center, axis=-1, keepdims=True))
    return center * lax.rsqrt(spread + eps_norm)

def gelu_tanh(values):
    return jax.nn.gelu(values, approximate=True)

def group_forward(tokens, mod_rows, weights):
    qkv_low, out_low, up_low, down_low, biases = weights
    group_size = mod_rows.shape[0]
    row_total = tokens.shape[0]
    per_token = jnp.repeat(mod_rows, L, axis=0)
    shift_attn = per_token[:, 0:D]
    scale_attn = per_token[:, D:2 * D]
    gate_attn = per_token[:, 2 * D:3 * D]
    shift_mlp = per_token[:, 3 * D:4 * D]
    scale_mlp = per_token[:, 4 * D:5 * D]
    gate_mlp = per_token[:, 5 * D:6 * D]
    norm_attn = layer_norm(tokens)
    attn_input = low(norm_attn * (1.0 + scale_attn) + shift_attn)
    projected = matmul(attn_input, qkv_low)
    query_low = low(low_back(projected[:, 0:D] + biases[0:D]))
    key_low = low(low_back(projected[:, D:2 * D]))
    value_low = low(low_back(projected[:, 2 * D:3 * D] + biases[D:2 * D]))
    head_shape = (group_size, L, H, HD)
    scores = jnp.einsum('gqhd,gkhd->ghqk', query_low.reshape(head_shape), key_low.reshape(head_shape), precision=highest) * HD ** (-0.5)
    scores = low_back(scores)
    row_max = lax.optimization_barrier(jnp.max(scores, axis=-1, keepdims=True))
    exp_scores = jnp.exp(scores - row_max)
    prob_rows = exp_scores / lax.optimization_barrier(jnp.sum(exp_scores, axis=-1, keepdims=True))
    head_out = jnp.einsum('ghqk,gkhd->gqhd', low(prob_rows), value_low.reshape(head_shape), precision=highest)
    head_out = low(low_back(head_out.reshape(row_total, D)))
    attn_value = low_back(matmul(head_out, out_low) + biases[2 * D:3 * D])
    residual_mid = tokens + gate_attn * attn_value
    mlp_input = low(layer_norm(residual_mid) * (1.0 + scale_mlp) + shift_mlp)
    up_value = low_back(matmul(mlp_input, up_low) + biases[3 * D:3 * D + FF])
    hidden = low(gelu_tanh(up_value))
    mlp_value = low_back(matmul(hidden, down_low) + biases[3 * D + FF:4 * D + FF])
    return residual_mid + gate_mlp * mlp_value

def forward(tokens_in, condition, qkv_weight, out_weight, up_weight, down_weight, ada_weight, bias_all):
    modulation = matmul(low(jax.nn.silu(condition)), low(ada_weight)) + bias_all[4 * D + FF:]
    weights = (low(qkv_weight).reshape(D, 3 * D), low(out_weight), low(up_weight), low(down_weight), bias_all)
    group_size = math.gcd(NLAT, 4)
    tokens = tokens_in.reshape(NLAT // group_size, group_size * L, D)
    mod_groups = modulation.reshape(NLAT // group_size, group_size, 6 * D)

    def run_group(pieces):
        return group_forward(pieces[0], pieces[1], weights)
    outputs = lax.map(jax.checkpoint(run_group), (tokens, mod_groups))
    return outputs.reshape(NLAT * L, D)

def adam_update(weight, gradient, first_old, second, step_rate):
    first_new = beta_one * first_old + (1.0 - beta_one) * gradient
    second_new = beta_two * second + (1.0 - beta_two) * gradient * gradient
    first_hat = first_new / (1.0 - beta_one ** STEP)
    second_hat = second_new / (1.0 - beta_two ** STEP)
    weight_new = weight - step_rate * (first_hat / (jnp.sqrt(second_hat) + adam_eps) + decay_rate * weight)
    return (first_new, second_new, weight_new)

def reference(tokens_in, condition, out_grad, qkv_weight, out_weight, up_weight, down_weight, ada_weight, bias_all, qkv_first, out_first, up_first, down_first, ada_first, bias_first, qkv_second, out_second, up_second, down_second, ada_second, bias_second):
    block_out, pullback = jax.vjp(forward, tokens_in, condition.astype(jnp.float32), qkv_weight, out_weight, up_weight, down_weight, ada_weight, bias_all)
    tokens_grad, condition_grad, qkv_grad, out_wgrad, up_wgrad, down_wgrad, ada_wgrad, bias_grad = pullback(out_grad)
    qkv_new = adam_update(qkv_weight, qkv_grad, qkv_first, qkv_second, 3.0 / math.sqrt(D))
    out_new = adam_update(out_weight, out_wgrad, out_first, out_second, 3.0 / math.sqrt(D // 4))
    up_new = adam_update(up_weight, up_wgrad, up_first, up_second, 3.0 / math.sqrt(D))
    down_new = adam_update(down_weight, down_wgrad, down_first, down_second, 3.0 / math.sqrt(FF))
    ada_new = adam_update(ada_weight, ada_wgrad, ada_first, ada_second, 3.0 / math.sqrt(D))
    bias_new = adam_update(bias_all, bias_grad, bias_first, bias_second, 0.9)
    return (block_out, tokens_grad, condition_grad, qkv_new[0], qkv_new[1], qkv_new[2], out_new[0], out_new[1], out_new[2], up_new[0], up_new[1], up_new[2], down_new[0], down_new[1], down_new[2], ada_new[0], ada_new[1], ada_new[2], bias_new[0], bias_new[1], bias_new[2])
```

```python
import math

import jax
import jax.numpy as jnp
import numpy as np
from jax import lax
from jax.experimental import pallas as pl
from jax.experimental.pallas import tpu as pltpu
from jax.sharding import PartitionSpec as P

D = 1024
HD = 64
FF = 4096
L = 1024
STEP = 10
LANES = 128
VMEM_BYTES = 48 * 1024 * 1024


eps_norm = 1e-06
beta_one = 0.9
beta_two = 0.95
adam_eps = 1e-08
decay_rate = 0.01
highest = lax.Precision.HIGHEST
both = ("dp", "tensor")


def halo_plan(device_count, row_count):
    by_size = {}
    for dst in range(device_count):
        low = dst * row_count // L * L
        high = -(-(dst + 1) * row_count // L) * L
        for src in range(low // row_count, -(-high // row_count)):
            start = max(low, src * row_count)
            stop = min(high, (src + 1) * row_count)
            if src != dst and start < stop:
                piece = (src, dst, start - src * row_count, start - low)
                by_size.setdefault(stop - start, []).append(piece)
    rounds = []
    for size in sorted(by_size, reverse=True):
        left = by_size[size]
        while left:
            taken, later, sources, targets = [], [], set(), set()
            for piece in left:
                if piece[0] in sources or piece[1] in targets:
                    later.append(piece)
                else:
                    taken.append(piece)
                    sources.add(piece[0])
                    targets.add(piece[1])
            rounds.append((size, taken))
            left = later
    return rounds


def window_latents(device_count, row_count):
    widths = [
        -(-(i + 1) * row_count // L) - i * row_count // L for i in range(device_count)
    ]
    return max(widths)


def look_up(table, index):
    return lax.dynamic_index_in_dim(jnp.asarray(np.array(table, np.int32)), index, 0, False)


def norm_parts(values):
    center = values - jnp.mean(values, axis=-1, keepdims=True)
    spread = jnp.mean(center * center, axis=-1, keepdims=True)
    inverse = lax.rsqrt(spread + eps_norm)
    return (center * inverse, inverse)


def norm_back(normed, inverse, cotangent):
    mean_grad = jnp.mean(cotangent, axis=-1, keepdims=True)
    mean_dot = jnp.mean(cotangent * normed, axis=-1, keepdims=True)
    return inverse * (cotangent - mean_grad - normed * mean_dot)


def gelu_tanh(values):
    return jax.nn.gelu(values, approximate=True)


def adam_update(weight, gradient, first_old, second, step_rate):
    first_new = beta_one * first_old + (1.0 - beta_one) * gradient
    second_new = beta_two * second + (1.0 - beta_two) * gradient * gradient
    first_hat = first_new / (1.0 - beta_one**STEP)
    second_hat = second_new / (1.0 - beta_two**STEP)
    weight_new = weight - step_rate * (
        first_hat / (jnp.sqrt(second_hat) + adam_eps) + decay_rate * weight
    )
    return (first_new, second_new, weight_new)


def dot_nt(left, right):
    return lax.dot_general(
        left, right, (((1,), (1,)), ((), ())), preferred_element_type=jnp.float32
    )


def dot_nn(left, right):
    return lax.dot_general(
        left, right, (((1,), (0,)), ((), ())), preferred_element_type=jnp.float32
    )


def dot_tn(left, right):
    return lax.dot_general(
        left, right, (((0,), (0,)), ((), ())), preferred_element_type=jnp.float32
    )


def head_masks():
    lane = lax.broadcasted_iota(jnp.int32, (1, LANES), 1)
    low_half = (lane < HD).astype(jnp.bfloat16)
    return (low_half, (lane >= HD).astype(jnp.bfloat16))


def forward_kernel(start_ref, query_ref, key_ref, value_ref, heads_ref, log_ref):
    masks = head_masks()

    @pl.loop(0, query_ref.shape[1] // LANES)
    def pair_step(pair):
        cols = pl.ds(pl.multiple_of(pair * LANES, LANES), LANES)
        query = query_ref[:, cols] * jnp.bfloat16(HD**-0.5)
        key = key_ref[:, cols]
        value_turned = value_ref[:, cols].T
        outs = []
        for half in range(2):
            scores = dot_nt(key, query * masks[half])
            row_max = jnp.max(scores, axis=0, keepdims=True)
            weights = jnp.exp(scores - row_max)
            row_sum = jnp.sum(weights, axis=0, keepdims=True)
            out = dot_nn(
                value_turned[half * HD : (half + 1) * HD], weights.astype(jnp.bfloat16)
            )
            outs.append(out / row_sum)
            log_ref[0, 0, pl.ds(2 * pair + half, 1), :] = row_max + jnp.log(row_sum)
        heads_ref[:, cols] = jnp.concatenate(outs, axis=0).T.astype(jnp.bfloat16)


def backward_kernel(
    start_ref, query_ref, key_ref, value_ref, grad_ref, log_ref, out_ref, key_acc, value_acc
):
    step = pl.program_id(1)
    block_rows, width = query_ref.shape
    block = start_ref[0] + step
    latent = block * block_rows // L
    rows = pl.ds(pl.multiple_of(latent * L, L), L)
    own = pl.ds(pl.multiple_of(block * block_rows, block_rows), block_rows)
    masks = head_masks()

    @pl.when(step == 0)
    def clear():
        key_acc[...] = jnp.zeros_like(key_acc)
        value_acc[...] = jnp.zeros_like(value_acc)
        out_ref[:, :width] = jnp.zeros((out_ref.shape[0], width), out_ref.dtype)

    @pl.loop(0, width // LANES)
    def pair_step(pair):
        cols = pl.ds(pl.multiple_of(pair * LANES, LANES), LANES)
        query = query_ref[:, cols] * jnp.bfloat16(HD**-0.5)
        grad = grad_ref[:, cols]
        key = key_ref[:, cols]
        value = value_ref[:, cols]
        key_turned = key.T
        probs, score_grads, query_grads = [], [], []
        for half in range(2):
            scores = dot_nt(key, query * masks[half])
            prob = jnp.exp(scores - log_ref[0, 0, pl.ds(2 * pair + half, 1), :])
            weighted = prob * dot_nt(value, grad * masks[half])
            row_dot = jnp.sum(weighted, axis=0, keepdims=True)
            score_grad = (weighted - prob * row_dot).astype(jnp.bfloat16)
            query_grads.append(
                dot_nn(key_turned[half * HD : (half + 1) * HD], score_grad)
            )
            probs.append(prob.astype(jnp.bfloat16))
            score_grads.append(score_grad)
        queries = [query * mask for mask in masks]
        grads = [grad * mask for mask in masks]
        if block_rows % LANES == 0:
            probs, score_grads = (
                [jnp.concatenate(probs, axis=1)],
                [jnp.concatenate(score_grads, axis=1)],
            )
            queries, grads = (
                [jnp.concatenate(queries, axis=0)],
                [jnp.concatenate(grads, axis=0)],
            )
        value_acc[rows, cols] += sum(dot_nn(a, b) for a, b in zip(probs, grads))
        key_acc[rows, cols] += sum(dot_nn(a, b) for a, b in zip(score_grads, queries))
        turned = jnp.concatenate(query_grads, axis=0).T * HD**-0.5
        out_ref[own, cols] = turned.astype(jnp.bfloat16)

    @pl.when(step == pl.num_programs(1) - 1)
    def finish():
        out_ref[:, width : 2 * width] = key_acc[...].astype(jnp.bfloat16)
        out_ref[:, 2 * width :] = value_acc[...].astype(jnp.bfloat16)


def qkv_specs(block_rows, width):
    return [
        pl.BlockSpec((block_rows, width), lambda h, b, start: (start[0] + b, 3 * h)),
        pl.BlockSpec(
            (L, width), lambda h, b, start: ((start[0] + b) * block_rows // L, 3 * h + 1)
        ),
        pl.BlockSpec(
            (L, width), lambda h, b, start: ((start[0] + b) * block_rows // L, 3 * h + 2)
        ),
    ]


def attend_forward(qkv_ext, start_block, block_rows, block_count, chunks):
    width = D // chunks
    chunk_heads = width // HD
    cost = 4 * block_rows * block_count * L * D
    return pl.pallas_call(
        forward_kernel,
        grid_spec=pltpu.PrefetchScalarGridSpec(
            num_scalar_prefetch=1,
            grid=(chunks, block_count),
            in_specs=qkv_specs(block_rows, width),
            out_specs=[
                pl.BlockSpec((block_rows, width), lambda h, b, start: (b, h)),
                pl.BlockSpec(
                    (1, 1, chunk_heads, block_rows), lambda h, b, start: (h, b, 0, 0)
                ),
            ],
        ),
        out_shape=[
            jax.ShapeDtypeStruct((block_rows * block_count, D), jnp.bfloat16),
            jax.ShapeDtypeStruct((chunks, block_count, chunk_heads, block_rows), jnp.float32),
        ],
        compiler_params=pltpu.CompilerParams(vmem_limit_bytes=VMEM_BYTES),
        cost_estimate=pl.CostEstimate(
            flops=4 * cost, bytes_accessed=qkv_ext.size * 4, transcendentals=cost // 4 // HD
        ),
        name="attend_forward",
    )(start_block, qkv_ext, qkv_ext, qkv_ext)


def attend_backward(qkv_ext, heads_grad, log_totals, start_block, block_rows, block_count, chunks):
    width = D // chunks
    chunk_heads = width // HD
    ext_rows = qkv_ext.shape[0]
    cost = 10 * block_rows * block_count * L * D
    return pl.pallas_call(
        backward_kernel,
        grid_spec=pltpu.PrefetchScalarGridSpec(
            num_scalar_prefetch=1,
            grid=(chunks, block_count),
            in_specs=qkv_specs(block_rows, width)
            + [
                pl.BlockSpec((block_rows, width), lambda h, b, start: (b, h)),
                pl.BlockSpec(
                    (1, 1, chunk_heads, block_rows), lambda h, b, start: (h, b, 0, 0)
                ),
            ],
            out_specs=pl.BlockSpec((ext_rows, 3 * width), lambda h, b, start: (0, h)),
            scratch_shapes=[
                pltpu.VMEM((ext_rows, width), jnp.float32),
                pltpu.VMEM((ext_rows, width), jnp.float32),
            ],
        ),
        out_shape=jax.ShapeDtypeStruct((ext_rows, 3 * D), jnp.bfloat16),
        compiler_params=pltpu.CompilerParams(vmem_limit_bytes=VMEM_BYTES),
        cost_estimate=pl.CostEstimate(
            flops=4 * cost, bytes_accessed=qkv_ext.size * 6, transcendentals=cost // 10 // HD
        ),
        name="attend_backward",
    )(start_block, qkv_ext, qkv_ext, qkv_ext, heads_grad, log_totals)


def gather_columns(shard):
    tensor_count = lax.axis_size("tensor")
    whole = lax.all_gather(shard, both, axis=0, tiled=False)
    whole = whole.reshape(-1, tensor_count, *shard.shape)
    return whole.transpose(0, 2, 1, 3).reshape(D, tensor_count * shard.shape[1])


def scatter_columns(grad):
    tensor_count = lax.axis_size("tensor")
    dp_count = lax.axis_size("dp")
    columns = grad.shape[1] // tensor_count
    parts = grad.reshape(dp_count, D // dp_count, tensor_count, columns).transpose(0, 2, 1, 3)
    parts = parts.reshape(dp_count * tensor_count, D // dp_count, columns)
    summed = lax.psum_scatter(parts, both, scatter_dimension=0, tiled=False)
    return summed.astype(jnp.float32)


def on_device(
    tokens_in,
    condition,
    out_grad,
    qkv_weight,
    out_weight,
    up_weight,
    down_weight,
    ada_weight,
    bias_all,
    qkv_first,
    out_first,
    up_first,
    down_first,
    ada_first,
    bias_first,
    qkv_second,
    out_second,
    up_second,
    down_second,
    ada_second,
    bias_second,
):
    tensor_count = lax.axis_size("tensor")
    dp_count = lax.axis_size("dp")
    device_count = dp_count * tensor_count
    dp_index = lax.axis_index("dp")
    device = dp_index * tensor_count + lax.axis_index("tensor")
    row_count = tokens_in.shape[0]
    latent_count = condition.shape[0]
    width = D // tensor_count
    block_rows = math.gcd(row_count, L)
    block_count = row_count // block_rows
    rounds = halo_plan(device_count, row_count)
    window = window_latents(device_count, row_count)
    dp_window = window_latents(dp_count, row_count * tensor_count)
    first_latents = [i * row_count // L for i in range(device_count)]
    dp_latents = [i * row_count * tensor_count // L for i in range(dp_count)]
    first_latent = look_up(first_latents, device)
    start_block = look_up(
        [i * row_count % L // block_rows for i in range(device_count)], device
    )

    qkv_whole = gather_columns(qkv_weight.astype(jnp.bfloat16).reshape(-1, 3 * width))
    out_whole = gather_columns(out_weight.astype(jnp.bfloat16).T)
    up_whole = gather_columns(up_weight.astype(jnp.bfloat16))
    down_whole = gather_columns(down_weight.astype(jnp.bfloat16).T)

    cond_value = condition.astype(jnp.float32)
    silu_low = jax.nn.silu(cond_value).astype(jnp.bfloat16)
    ada_low = ada_weight.astype(jnp.bfloat16)
    picked = [
        min(first + w, latent_count - 1) for first in dp_latents for w in range(dp_window)
    ]
    silu_picked = jnp.stack([silu_low[latent] for latent in picked])
    ada_part = dot_nn(silu_picked, ada_low).reshape(dp_count, dp_window, 6 * D)
    ada_parts = lax.all_to_all(ada_part, "dp", split_axis=0, concat_axis=0, tiled=True)
    mod_dp = jnp.sum(ada_parts, axis=0) + bias_all[4 * D + FF :]
    mod_dp = jnp.concatenate([mod_dp, jnp.zeros((window, 6 * D), jnp.float32)])
    mod_window = lax.dynamic_slice_in_dim(
        mod_dp, first_latent - look_up(dp_latents, dp_index), window, 0
    )
    block_latent = (start_block + jnp.arange(block_count, dtype=jnp.int32)) * block_rows // L
    latent_pick = (
        block_latent[None, :] == jnp.arange(window, dtype=jnp.int32)[:, None]
    ).astype(jnp.float32)
    mod_blocks = jnp.sum(latent_pick[:, :, None] * mod_window[:, None, :], axis=0)
    mod_blocks = mod_blocks.reshape(block_count, 1, 6 * D)
    shift_attn, scale_attn, gate_attn, shift_mlp, scale_mlp, gate_mlp = (
        mod_blocks[:, :, i * D : (i + 1) * D] for i in range(6)
    )

    def in_blocks(values):
        return values.reshape(block_count, block_rows, -1)

    def in_rows(values):
        return values.reshape(row_count, -1)

    def latent_sums(values):
        return jnp.sum(latent_pick[:, :, None] * jnp.sum(values, axis=1)[None], axis=1)

    tokens = in_blocks(tokens_in)
    cotangent = in_blocks(out_grad)
    norm_attn, inverse_attn = norm_parts(tokens)
    attn_input = (norm_attn * (1.0 + scale_attn) + shift_attn).astype(jnp.bfloat16)

    attn_ext = jnp.zeros((window * L // block_rows, block_rows, D), jnp.bfloat16)
    places = []
    for size, pieces in rounds:
        source = [0] * device_count
        target = [i * row_count % L // block_rows for i in range(device_count)]
        for src, dst, src_row, dst_row in pieces:
            source[src] = src_row // block_rows
            target[dst] = dst_row // block_rows
        places.append((look_up(source, device), look_up(target, device)))
    for (size, pieces), (source, target) in zip(rounds, places):
        sent = lax.dynamic_slice_in_dim(attn_input, source, size // block_rows, 0)
        got = lax.ppermute(sent, both, [(piece[0], piece[1]) for piece in pieces])
        attn_ext = lax.dynamic_update_slice_in_dim(attn_ext, got, target, 0)
    attn_ext = lax.dynamic_update_slice_in_dim(attn_ext, attn_input, start_block, 0)
    attn_ext = attn_ext.reshape(window * L, D)

    bias_chunks = jnp.stack(
        [
            bias_all[:D].reshape(tensor_count, width),
            jnp.zeros((tensor_count, width), jnp.float32),
            bias_all[D : 2 * D].reshape(tensor_count, width),
        ],
        axis=1,
    ).reshape(3 * D)
    qkv_ext = (dot_nn(attn_ext, qkv_whole) + bias_chunks).astype(jnp.bfloat16)
    starts = start_block.reshape(1)
    head_low, log_totals = attend_forward(
        qkv_ext, starts, block_rows, block_count, tensor_count
    )
    attn_value = in_blocks(dot_nt(head_low, out_whole) + bias_all[2 * D : 3 * D])
    residual_mid = tokens + gate_attn * attn_value
    norm_mlp, inverse_mlp = norm_parts(residual_mid)
    mlp_low = in_rows((norm_mlp * (1.0 + scale_mlp) + shift_mlp).astype(jnp.bfloat16))
    mlp_grad = in_rows((cotangent * gate_mlp).astype(jnp.bfloat16))

    up_value = dot_nn(mlp_low, up_whole) + bias_all[3 * D : 3 * D + FF]
    hidden_low = gelu_tanh(up_value).astype(jnp.bfloat16)
    mlp_value = in_blocks(dot_nt(hidden_low, down_whole) + bias_all[3 * D + FF : 4 * D + FF])
    hidden_grad = dot_nn(mlp_grad, down_whole)
    unused, gelu_pull = jax.vjp(gelu_tanh, up_value)
    up_grad = gelu_pull(hidden_grad)[0].astype(jnp.bfloat16)
    down_wgrad = dot_tn(mlp_grad, hidden_low).astype(jnp.bfloat16)
    up_wgrad = dot_tn(mlp_low, up_grad).astype(jnp.bfloat16)
    mlp_norm_grad = in_blocks(dot_nt(up_grad, up_whole))
    block_out = in_rows(residual_mid + gate_mlp * mlp_value)
    mid_grad = cotangent + norm_back(norm_mlp, inverse_mlp, mlp_norm_grad * (1.0 + scale_mlp))
    attn_grad = in_rows((mid_grad * gate_attn).astype(jnp.bfloat16))
    out_wgrad = dot_tn(attn_grad, head_low).astype(jnp.bfloat16)
    heads_grad = dot_nn(attn_grad, out_whole).astype(jnp.bfloat16)

    early = jnp.concatenate(
        [
            jnp.sum(attn_grad.astype(jnp.float32), axis=0),
            jnp.sum(up_grad.astype(jnp.float32), axis=0),
            jnp.sum(mlp_grad.astype(jnp.float32), axis=0),
            latent_sums(mid_grad * attn_value).reshape(-1),
            latent_sums(mlp_norm_grad).reshape(-1),
            latent_sums(mlp_norm_grad * norm_mlp).reshape(-1),
            latent_sums(cotangent * mlp_value).reshape(-1),
        ]
    )
    early_all = lax.all_gather(early.reshape(-1, LANES), both, axis=0, tiled=False)
    early_all = early_all.reshape(device_count, -1)

    qkv_grad = attend_backward(
        qkv_ext, heads_grad, log_totals, starts, block_rows, block_count, tensor_count
    )
    qkv_wgrad = dot_tn(attn_ext, qkv_grad).astype(jnp.bfloat16)
    norm_grad_ext = dot_nt(qkv_grad, qkv_whole).reshape(-1, block_rows, D)
    attn_norm_grad = lax.dynamic_slice_in_dim(norm_grad_ext, start_block, block_count, 0)
    for (size, pieces), (source, target) in zip(rounds, places):
        count = size // block_rows
        sent = lax.dynamic_slice_in_dim(norm_grad_ext, target, count, 0).astype(jnp.bfloat16)
        got = lax.ppermute(sent, both, [(piece[1], piece[0]) for piece in pieces])
        old = lax.dynamic_slice_in_dim(attn_norm_grad, source, count, 0)
        attn_norm_grad = lax.dynamic_update_slice_in_dim(
            attn_norm_grad, old + got.astype(jnp.float32), source, 0
        )
    tokens_grad = in_rows(
        mid_grad + norm_back(norm_attn, inverse_attn, attn_norm_grad * (1.0 + scale_attn))
    )
    qkv_sums = jnp.sum(qkv_grad.astype(jnp.float32), axis=0).reshape(tensor_count, 3, width)
    late = jnp.concatenate(
        [
            qkv_sums[:, 0].reshape(-1),
            qkv_sums[:, 2].reshape(-1),
            latent_sums(attn_norm_grad).reshape(-1),
            latent_sums(attn_norm_grad * norm_attn).reshape(-1),
        ]
    )
    late_all = lax.all_gather(late.reshape(-1, LANES), both, axis=0, tiled=False)
    late_all = late_all.reshape(device_count, -1)

    spread = np.zeros((latent_count, device_count, window), np.float32)
    for i, first in enumerate(first_latents):
        for w in range(window):
            if first + w < latent_count:
                spread[first + w, i, w] = 1.0
    spread = jnp.asarray(spread.reshape(latent_count, -1))

    def latent_totals(gathered):
        terms = gathered.reshape(device_count * window, D)
        return jnp.dot(spread, terms, precision=highest, preferred_element_type=jnp.float32)

    early_bias = 2 * D + FF
    mod_grads = [
        latent_totals(late_all[:, 2 * D + i * window * D : 2 * D + (i + 1) * window * D])
        for i in range(2)
    ] + [
        latent_totals(
            early_all[:, early_bias + i * window * D : early_bias + (i + 1) * window * D]
        )
        for i in range(4)
    ]
    mod_grad = jnp.concatenate(mod_grads, axis=1)
    bias_grad = jnp.concatenate(
        [
            jnp.sum(late_all[:, : 2 * D], axis=0),
            jnp.sum(early_all[:, :early_bias], axis=0),
            jnp.sum(mod_grad, axis=0),
        ]
    )
    ada_wgrad = jnp.dot(
        silu_low.astype(jnp.float32).T,
        mod_grad,
        precision=highest,
        preferred_element_type=jnp.float32,
    )
    cond_inner = jnp.dot(
        mod_grad,
        ada_low.astype(jnp.float32).T,
        precision=highest,
        preferred_element_type=jnp.float32,
    )
    unused, silu_pull = jax.vjp(jax.nn.silu, cond_value)
    condition_grad = silu_pull(cond_inner)[0]
    down_summed = scatter_columns(down_wgrad).T
    up_summed = scatter_columns(up_wgrad)
    out_summed = scatter_columns(out_wgrad).T
    qkv_summed = scatter_columns(qkv_wgrad).reshape(qkv_weight.shape)
    qkv_new = adam_update(qkv_weight, qkv_summed, qkv_first, qkv_second, 3.0 / math.sqrt(D))
    out_new = adam_update(out_weight, out_summed, out_first, out_second, 3.0 / math.sqrt(D // 4))
    up_new = adam_update(up_weight, up_summed, up_first, up_second, 3.0 / math.sqrt(D))
    down_new = adam_update(down_weight, down_summed, down_first, down_second, 3.0 / math.sqrt(FF))
    ada_new = adam_update(ada_weight, ada_wgrad, ada_first, ada_second, 3.0 / math.sqrt(D))
    bias_new = adam_update(bias_all, bias_grad, bias_first, bias_second, 0.9)
    return (
        block_out,
        tokens_grad,
        condition_grad,
        *qkv_new,
        *out_new,
        *up_new,
        *down_new,
        *ada_new,
        *bias_new,
    )


def solution(mesh):
    weights = (
        P("dp", None, "tensor"),
        P("tensor", "dp"),
        P("dp", "tensor"),
        P("tensor", "dp"),
        P("dp", None),
        P(),
    )
    tokens = P(both, None)
    return jax.shard_map(
        on_device,
        mesh=mesh,
        in_specs=(tokens, P(None, "dp"), tokens, *weights, *weights, *weights),
        out_specs=(tokens, tokens, P(None, "dp"))
        + tuple(spec for spec in weights for unused in range(3)),
        check_vma=False,
    )
```

```python
import math

import jax
import jax.numpy as jnp
import numpy as np
from jax import lax
from jax.experimental import pallas as pl
from jax.experimental.pallas import tpu as pltpu
from jax.sharding import PartitionSpec as P

D = 1024
HD = 64
FF = 4096
L = 1024
STEP = 10
LANES = 128
VMEM_BYTES = 48 * 1024 * 1024


eps_norm = 1e-06
beta_one = 0.9
beta_two = 0.95
adam_eps = 1e-08
decay_rate = 0.01
highest = lax.Precision.HIGHEST
both = ("dp", "tensor")


def halo_plan(device_count, row_count):
    by_size = {}
    for dst in range(device_count):
        low = dst * row_count // L * L
        high = -(-(dst + 1) * row_count // L) * L
        for src in range(low // row_count, -(-high // row_count)):
            start = max(low, src * row_count)
            stop = min(high, (src + 1) * row_count)
            if src != dst and start < stop:
                piece = (src, dst, start - src * row_count, start - low)
                by_size.setdefault(stop - start, []).append(piece)
    rounds = []
    for size in sorted(by_size, reverse=True):
        left = by_size[size]
        while left:
            taken, later, sources, targets = [], [], set(), set()
            for piece in left:
                if piece[0] in sources or piece[1] in targets:
                    later.append(piece)
                else:
                    taken.append(piece)
                    sources.add(piece[0])
                    targets.add(piece[1])
            rounds.append((size, taken))
            left = later
    return rounds


def window_latents(device_count, row_count):
    widths = [
        -(-(i + 1) * row_count // L) - i * row_count // L for i in range(device_count)
    ]
    return max(widths)


def look_up(table, index):
    return lax.dynamic_index_in_dim(jnp.asarray(np.array(table, np.int32)), index, 0, False)


def norm_parts(values):
    center = values - jnp.mean(values, axis=-1, keepdims=True)
    spread = jnp.mean(center * center, axis=-1, keepdims=True)
    inverse = lax.rsqrt(spread + eps_norm)
    return (center * inverse, inverse)


def norm_back(normed, inverse, cotangent):
    mean_grad = jnp.mean(cotangent, axis=-1, keepdims=True)
    mean_dot = jnp.mean(cotangent * normed, axis=-1, keepdims=True)
    return inverse * (cotangent - mean_grad - normed * mean_dot)


def gelu_tanh(values):
    return jax.nn.gelu(values, approximate=True)


def adam_update(weight, gradient, first_old, second, step_rate):
    first_new = beta_one * first_old + (1.0 - beta_one) * gradient
    second_new = beta_two * second + (1.0 - beta_two) * gradient * gradient
    first_hat = first_new / (1.0 - beta_one**STEP)
    second_hat = second_new / (1.0 - beta_two**STEP)
    weight_new = weight - step_rate * (
        first_hat / (jnp.sqrt(second_hat) + adam_eps) + decay_rate * weight
    )
    return (first_new, second_new, weight_new)


def dot_nt(left, right):
    return lax.dot_general(
        left, right, (((1,), (1,)), ((), ())), preferred_element_type=jnp.float32
    )


def dot_nn(left, right):
    return lax.dot_general(
        left, right, (((1,), (0,)), ((), ())), preferred_element_type=jnp.float32
    )


def dot_tn(left, right):
    return lax.dot_general(
        left, right, (((0,), (0,)), ((), ())), preferred_element_type=jnp.float32
    )


def head_masks():
    lane = lax.broadcasted_iota(jnp.int32, (1, LANES), 1)
    low_half = (lane < HD).astype(jnp.bfloat16)
    return (low_half, (lane >= HD).astype(jnp.bfloat16))


def forward_kernel(start_ref, query_ref, key_ref, value_ref, heads_ref, log_ref):
    masks = head_masks()
    pairs = query_ref.shape[1] // LANES
    group = 2 if pairs % 2 == 0 else 1

    @pl.loop(0, pairs // group)
    def group_step(step):
        scores, turned = [], []
        for i in range(group):
            cols = pl.ds(pl.multiple_of((step * group + i) * LANES, LANES), LANES)
            query = query_ref[:, cols] * jnp.bfloat16(HD**-0.5)
            scores += [dot_nt(key_ref[:, cols], query * mask) for mask in masks]
            turned.append(value_ref[:, cols].T)
        for i in range(group):
            pair = step * group + i
            outs = []
            for half in range(2):
                score = scores[2 * i + half]
                row_max = jnp.max(score, axis=0, keepdims=True)
                weights = jnp.exp(score - row_max)
                row_sum = jnp.sum(weights, axis=0, keepdims=True)
                out = dot_nn(
                    turned[i][half * HD : (half + 1) * HD], weights.astype(jnp.bfloat16)
                )
                outs.append(out / row_sum)
                log_ref[0, pl.ds(2 * pair + half, 1), :] = row_max + jnp.log(row_sum)
            cols = pl.ds(pl.multiple_of(pair * LANES, LANES), LANES)
            heads_ref[:, cols] = jnp.concatenate(outs, axis=0).T.astype(jnp.bfloat16)


def backward_kernel(
    start_ref,
    query_ref,
    key_ref,
    value_ref,
    heads_ref,
    grad_ref,
    log_ref,
    out_ref,
    key_acc,
    value_acc,
):
    step = pl.program_id(0)
    block_rows, width = query_ref.shape
    block = start_ref[0] + step
    latent = block * block_rows // L
    own = pl.ds(pl.multiple_of(block * block_rows, block_rows), block_rows)
    masks = head_masks()
    key_rows = L // 2

    @pl.when(step == 0)
    def clear():
        key_acc[...] = jnp.zeros_like(key_acc)
        value_acc[...] = jnp.zeros_like(value_acc)
        out_ref[:, :width] = jnp.zeros((out_ref.shape[0], width), out_ref.dtype)

    @pl.loop(0, width // LANES)
    def pair_step(pair):
        cols = pl.ds(pl.multiple_of(pair * LANES, LANES), LANES)
        query = query_ref[:, cols] * jnp.bfloat16(HD**-0.5)
        grad = grad_ref[:, cols]
        dots = (grad.astype(jnp.float32) * heads_ref[:, cols].astype(jnp.float32)).T
        key_turned = key_ref[:, cols].T
        queries = [query * mask for mask in masks]
        grads = [grad * mask for mask in masks]
        logs = [log_ref[0, pl.ds(2 * pair + half, 1), :] for half in range(2)]
        row_dots = [
            jnp.sum(dots[half * HD : (half + 1) * HD], axis=0, keepdims=True) for half in range(2)
        ]
        joined = block_rows % LANES == 0
        if joined:
            queries, grads = (
                [jnp.concatenate(queries, axis=0)],
                [jnp.concatenate(grads, axis=0)],
            )
            logs, row_dots = (
                [jnp.concatenate(logs, axis=1)],
                [jnp.concatenate(row_dots, axis=1)],
            )
        query_grads = [0.0, 0.0]
        for start in range(0, L, key_rows):
            key = key_ref[start : start + key_rows, cols]
            value = value_ref[start : start + key_rows, cols]
            value_part = key_part = 0.0
            for i in range(len(queries)):
                prob = jnp.exp(dot_nt(key, queries[i]) - logs[i])
                prob_grad = dot_nt(value, grads[i])
                score_grad = (prob * (prob_grad - row_dots[i])).astype(jnp.bfloat16)
                value_part += dot_nn(prob.astype(jnp.bfloat16), grads[i])
                key_part += dot_nn(score_grad, queries[i])
                for half in range(2) if joined else (i,):
                    mine = score_grad
                    if joined:
                        mine = score_grad[:, half * block_rows : (half + 1) * block_rows]
                    turned = key_turned[half * HD : (half + 1) * HD, start : start + key_rows]
                    query_grads[half] += dot_nn(turned, mine)
            rows = pl.ds(pl.multiple_of(latent * L + start, key_rows), key_rows)
            value_acc[rows, cols] += value_part
            key_acc[rows, cols] += key_part
        turned = jnp.concatenate(query_grads, axis=0).T * HD**-0.5
        out_ref[own, cols] = turned.astype(jnp.bfloat16)

    @pl.when(step == pl.num_programs(0) - 1)
    def finish():
        out_ref[:, width : 2 * width] = key_acc[...].astype(jnp.bfloat16)
        out_ref[:, 2 * width :] = value_acc[...].astype(jnp.bfloat16)


def qkv_specs(block_rows, width):
    return [
        pl.BlockSpec((block_rows, width), lambda b, start: (start[0] + b, 0)),
        pl.BlockSpec((L, width), lambda b, start: ((start[0] + b) * block_rows // L, 1)),
        pl.BlockSpec((L, width), lambda b, start: ((start[0] + b) * block_rows // L, 2)),
    ]


def attend_forward(qkv_ext, start_block, block_rows, block_count):
    width = qkv_ext.shape[1] // 3
    heads = width // HD
    cost = 4 * block_rows * block_count * L * width
    return pl.pallas_call(
        forward_kernel,
        grid_spec=pltpu.PrefetchScalarGridSpec(
            num_scalar_prefetch=1,
            grid=(block_count,),
            in_specs=qkv_specs(block_rows, width),
            out_specs=[
                pl.BlockSpec((block_rows, width), lambda b, start: (b, 0)),
                pl.BlockSpec((1, heads, block_rows), lambda b, start: (b, 0, 0)),
            ],
        ),
        out_shape=[
            jax.ShapeDtypeStruct((block_rows * block_count, width), jnp.bfloat16),
            jax.ShapeDtypeStruct((block_count, heads, block_rows), jnp.float32),
        ],
        compiler_params=pltpu.CompilerParams(vmem_limit_bytes=VMEM_BYTES),
        cost_estimate=pl.CostEstimate(
            flops=4 * cost, bytes_accessed=qkv_ext.size * 4, transcendentals=cost // 4 // HD
        ),
        name="attend_forward",
    )(start_block, qkv_ext, qkv_ext, qkv_ext)


def attend_backward(
    qkv_ext, heads_low, heads_grad, log_totals, start_block, block_rows, block_count
):
    ext_rows, width = qkv_ext.shape[0], qkv_ext.shape[1] // 3
    heads = width // HD
    cost = 10 * block_rows * block_count * L * width
    return pl.pallas_call(
        backward_kernel,
        grid_spec=pltpu.PrefetchScalarGridSpec(
            num_scalar_prefetch=1,
            grid=(block_count,),
            in_specs=qkv_specs(block_rows, width)
            + [
                pl.BlockSpec((block_rows, width), lambda b, start: (b, 0)),
                pl.BlockSpec((block_rows, width), lambda b, start: (b, 0)),
                pl.BlockSpec((1, heads, block_rows), lambda b, start: (b, 0, 0)),
            ],
            out_specs=pl.BlockSpec((ext_rows, 3 * width), lambda b, start: (0, 0)),
            scratch_shapes=[
                pltpu.VMEM((ext_rows, width), jnp.float32),
                pltpu.VMEM((ext_rows, width), jnp.float32),
            ],
        ),
        out_shape=jax.ShapeDtypeStruct((ext_rows, 3 * width), jnp.bfloat16),
        compiler_params=pltpu.CompilerParams(vmem_limit_bytes=VMEM_BYTES),
        cost_estimate=pl.CostEstimate(
            flops=4 * cost, bytes_accessed=qkv_ext.size * 6, transcendentals=cost // 10 // HD
        ),
        name="attend_backward",
    )(start_block, qkv_ext, qkv_ext, qkv_ext, heads_low, heads_grad, log_totals)


def axis_bits():
    dp_bits = lax.axis_size("dp").bit_length() - 1
    tensor_bits = lax.axis_size("tensor").bit_length() - 1
    z_bits = [("dp", bit) for bit in (dp_bits - 1, dp_bits - 2)]
    x_bits = [("dp", bit) for bit in range(dp_bits - 3, 0, -1)]
    y_bits = [("tensor", bit) for bit in range(tensor_bits - 1, -1, -1)]
    return z_bits, x_bits, y_bits


def own_bit(place):
    return lax.axis_index(place[0]) >> place[1] & 1


def swap(values, place):
    axis, bit = place
    route = [(i, i ^ 1 << bit) for i in range(lax.axis_size(axis))]
    return lax.ppermute(values, axis, route)


def add_low(kept, got):
    return (kept.astype(jnp.float32) + got.astype(jnp.float32)).astype(jnp.bfloat16)


def pick_half(values, axis, bit):
    return lax.dynamic_index_in_dim(values, bit, axis, False)


class SumChain:
    def __init__(self, groups):
        dp_count = lax.axis_size("dp")
        rows, columns = D // dp_count, groups[0][0].shape[1]
        z_bits, x_bits, y_bits = axis_bits()
        parts = [part.reshape(dp_count // 2, 2, rows, columns) for group in groups for part in group]
        places = ["group"] + y_bits + z_bits + x_bits
        self.shape = (len(groups),) + (2,) * (len(places) - 1) + (rows, columns)
        self.parts = parts
        self.places = places
        self.stages = [[("dp", 0)]]
        self.stages += [list(both) for both in zip(x_bits + y_bits, y_bits + x_bits)]
        self.stages += [[z_bits[0]], [z_bits[1]]]
        self.z_bits = z_bits
        self.stage = 0

    def done(self):
        return self.stage == len(self.stages)

    def sends(self):
        stage = self.stages[self.stage]
        if self.stage == 0:
            bit = own_bit(stage[0])
            self.kept = [pick_half(part, 1, bit) for part in self.parts]
            return [pick_half(part, 1, 1 - bit) for part in self.parts]
        if self.stage == len(self.stages) - 2:
            upper = own_bit(stage[0]) == 1
            first, second = self.halves
            self.kept = [jnp.where(upper, second, first)]
            return [jnp.where(upper, first, second)]
        sent, self.kept = [], []
        for i, place in enumerate(stage):
            axis, bit = self.labels[i].index(place), own_bit(place)
            sent.append(pick_half(self.halves[i], axis, 1 - bit))
            self.kept.append(pick_half(self.halves[i], axis, bit))
            self.labels[i] = [label for label in self.labels[i] if label != place]
        return sent

    def swap(self, sent):
        places = self.stages[self.stage]
        if self.stage == 0:
            places = places * len(sent)
        return [swap(values, place) for values, place in zip(sent, places)]

    def receive(self, got):
        self.stage += 1
        if self.stage == 1:
            self.kept, got = [jnp.stack(self.kept)], [jnp.stack(got)]
        if self.done():
            self.result = self.kept[0].astype(jnp.float32) + got[0].astype(jnp.float32)
            return
        totals = [add_low(kept, part) for kept, part in zip(self.kept, got)]
        if self.stage == 1:
            total = totals[0].reshape(self.shape)
            high = self.places.index(self.z_bits[0])
            rest = [place for place in self.places if place != self.z_bits[0]]
            totals = [lax.index_in_dim(total, i, high, False) for i in range(2)]
            self.labels = [rest, rest]
        elif self.stage == len(self.stages) - 1:
            self.labels = [["group", self.z_bits[1]]]
        self.halves = totals


class GatherChain:
    def __init__(self, values):
        z_bits, x_bits, y_bits = axis_bits()
        self.values, self.order = values[None], np.zeros((1,), np.int64)
        self.stages = z_bits + x_bits + y_bits + [("dp", 0)]
        self.stage = 0

    def done(self):
        return self.stage == len(self.stages)

    def sends(self):
        return [self.values]

    def swap(self, sent):
        return [swap(sent[0], self.stages[self.stage])]

    def receive(self, got):
        place = self.stages[self.stage]
        upper = own_bit(place) == 1
        self.values = jnp.concatenate(
            [jnp.where(upper, got[0], self.values), jnp.where(upper, self.values, got[0])]
        )
        weight = (lax.axis_size("tensor") if place[0] == "dp" else 1) << place[1]
        self.order = np.concatenate([self.order, self.order + weight])
        self.stage += 1


class Received:
    def __init__(self, values):
        self.values, self.got = values, None

    def done(self):
        return self.got is not None

    def sends(self):
        return self.values

    def swap(self, sent):
        return sent

    def receive(self, got):
        self.got = got


def advance(chains):
    chains = [chain for chain in chains if not chain.done()]
    got = lax.optimization_barrier([chain.swap(chain.sends()) for chain in chains])
    for chain, values in zip(chains, got):
        chain.receive(values)


def beside(chains, work, operand):
    chains = [chain for chain in chains if not chain.done()]
    operand, sent = lax.optimization_barrier((operand, [chain.sends() for chain in chains]))
    got = [chain.swap(values) for chain, values in zip(chains, sent)]
    result, got = lax.optimization_barrier((work(operand), got))
    for chain, values in zip(chains, got):
        chain.receive(values)
    return result


def gather_rows(shard):
    whole = lax.all_gather(shard, ("tensor", "dp"), axis=0, tiled=True)
    tensor_count = lax.axis_size("tensor")
    return whole.reshape(tensor_count, D, shard.shape[1])


def on_device(
    tokens_in,
    condition,
    out_grad,
    qkv_weight,
    out_weight,
    up_weight,
    down_weight,
    ada_weight,
    bias_all,
    qkv_first,
    out_first,
    up_first,
    down_first,
    ada_first,
    bias_first,
    qkv_second,
    out_second,
    up_second,
    down_second,
    ada_second,
    bias_second,
):
    tensor_count = lax.axis_size("tensor")
    dp_count = lax.axis_size("dp")
    device_count = dp_count * tensor_count
    dp_index = lax.axis_index("dp")
    device = dp_index * tensor_count + lax.axis_index("tensor")
    row_count = tokens_in.shape[0]
    latent_count = condition.shape[0]
    width = D // tensor_count
    block_rows = math.gcd(row_count, L)
    block_count = row_count // block_rows
    rounds = halo_plan(device_count, row_count)
    window = window_latents(device_count, row_count)
    dp_window = window_latents(dp_count, row_count * tensor_count)
    first_latents = [i * row_count // L for i in range(device_count)]
    dp_latents = [i * row_count * tensor_count // L for i in range(dp_count)]
    first_latent = look_up(first_latents, device)
    start_block = look_up(
        [i * row_count % L // block_rows for i in range(device_count)], device
    )

    hidden = FF // tensor_count
    chunks = range(tensor_count)
    attn_shard = jnp.concatenate(
        [
            qkv_weight.astype(jnp.bfloat16).reshape(-1, 3 * width),
            out_weight.astype(jnp.bfloat16).T,
        ],
        axis=1,
    )
    attn_whole = gather_rows(attn_shard)
    qkv_whole = [attn_whole[h, :, : 3 * width] for h in chunks]
    out_whole = [attn_whole[h, :, 3 * width :] for h in chunks]
    mlp_shard = jnp.concatenate(
        [up_weight.astype(jnp.bfloat16), down_weight.astype(jnp.bfloat16).T], axis=1
    )
    mlp_whole = gather_rows(mlp_shard)
    up_whole = [mlp_whole[h, :, :hidden] for h in chunks]
    down_whole = [mlp_whole[h, :, hidden:] for h in chunks]

    cond_value = condition.astype(jnp.float32)
    silu_low = jax.nn.silu(cond_value).astype(jnp.bfloat16)
    ada_low = ada_weight.astype(jnp.bfloat16)
    picked = [min(first, latent_count - dp_window) for first in dp_latents]
    silu_picked = jnp.concatenate([silu_low[first : first + dp_window] for first in picked])
    ada_part = dot_nn(silu_picked, ada_low).reshape(dp_count, dp_window, 6 * D)

    def in_blocks(values):
        return values.reshape(block_count, block_rows, -1)

    def in_rows(values):
        return values.reshape(row_count, -1)

    tokens = in_blocks(tokens_in)
    cotangent = in_blocks(out_grad)
    norm_attn, inverse_attn = norm_parts(tokens)
    ada_part, norm_low = lax.optimization_barrier((ada_part, norm_attn.astype(jnp.bfloat16)))
    norm_ext = jnp.zeros((window * L // block_rows, block_rows, D), jnp.bfloat16)
    places = []
    for size, pieces in rounds:
        source = [0] * device_count
        target = [i * row_count % L // block_rows for i in range(device_count)]
        for src, dst, src_row, dst_row in pieces:
            source[src] = src_row // block_rows
            target[dst] = dst_row // block_rows
        places.append((look_up(source, device), look_up(target, device)))
    for (size, pieces), (source, target) in zip(rounds, places):
        sent = lax.dynamic_slice_in_dim(norm_low, source, size // block_rows, 0)
        got = lax.ppermute(sent, both, [(piece[0], piece[1]) for piece in pieces])
        norm_ext = lax.dynamic_update_slice_in_dim(norm_ext, got, target, 0)
    norm_ext = lax.dynamic_update_slice_in_dim(norm_ext, norm_low, start_block, 0)

    ada_parts = lax.all_to_all(ada_part, "dp", split_axis=0, concat_axis=0, tiled=True)
    mod_dp = jnp.sum(ada_parts, axis=0) + bias_all[4 * D + FF :]
    mod_dp = jnp.concatenate([mod_dp, jnp.zeros((window, 6 * D), jnp.float32)])
    mod_window = lax.dynamic_slice_in_dim(
        mod_dp, first_latent - look_up(picked, dp_index), window, 0
    )
    block_latent = (start_block + jnp.arange(block_count, dtype=jnp.int32)) * block_rows // L
    latent_pick = (
        block_latent[None, :] == jnp.arange(window, dtype=jnp.int32)[:, None]
    ).astype(jnp.float32)
    mod_blocks = jnp.sum(latent_pick[:, :, None] * mod_window[:, None, :], axis=0)
    mod_blocks = mod_blocks.reshape(block_count, 1, 6 * D)
    shift_attn, scale_attn, gate_attn, shift_mlp, scale_mlp, gate_mlp = (
        mod_blocks[:, :, i * D : (i + 1) * D] for i in range(6)
    )

    def latent_sums(values):
        return jnp.sum(latent_pick[:, :, None] * jnp.sum(values, axis=1)[None], axis=1)

    norm_ext = norm_ext.reshape(window, L, D)
    attn_ext = (
        norm_ext.astype(jnp.float32) * (1.0 + mod_window[:, None, D : 2 * D])
        + mod_window[:, None, :D]
    ).astype(jnp.bfloat16)
    attn_own = (norm_attn * (1.0 + scale_attn) + shift_attn).astype(jnp.bfloat16)
    attn_ext = lax.dynamic_update_slice_in_dim(
        attn_ext.reshape(-1, block_rows, D), attn_own, start_block, 0
    ).reshape(window * L, D)

    starts = start_block.reshape(1)
    qkv_ext, head_low, log_totals = [], [], []
    for h in chunks:
        own = slice(h * width, (h + 1) * width)
        bias = jnp.concatenate(
            [bias_all[:D][own], jnp.zeros((width,), jnp.float32), bias_all[D : 2 * D][own]]
        )
        qkv_ext.append((dot_nn(attn_ext, qkv_whole[h]) + bias).astype(jnp.bfloat16))
        heads, logs = attend_forward(qkv_ext[h], starts, block_rows, block_count)
        head_low.append(heads)
        log_totals.append(logs)
    attn_value = sum(dot_nt(head_low[h], out_whole[h]) for h in chunks)
    attn_value = in_blocks(attn_value + bias_all[2 * D : 3 * D])
    residual_mid = tokens + gate_attn * attn_value
    norm_mlp, inverse_mlp = norm_parts(residual_mid)
    mlp_low = in_rows((norm_mlp * (1.0 + scale_mlp) + shift_mlp).astype(jnp.bfloat16))
    mlp_grad = in_rows((cotangent * gate_mlp).astype(jnp.bfloat16))

    up_values = [
        dot_nn(mlp_low, up_whole[h]) + bias_all[3 * D + h * hidden : 3 * D + (h + 1) * hidden]
        for h in chunks
    ]
    hidden_low = [gelu_tanh(up_value).astype(jnp.bfloat16) for up_value in up_values]
    down_sum = SumChain([[dot_tn(mlp_grad, part).astype(jnp.bfloat16) for part in hidden_low]])

    def up_backward(grad):
        grads, sums = [], []
        for h in chunks:
            unused, gelu_pull = jax.vjp(gelu_tanh, up_values[h])
            part = gelu_pull(dot_nn(grad, down_whole[h]))[0].astype(jnp.bfloat16)
            grads.append(part)
            sums.append(jnp.sum(part.astype(jnp.float32), axis=0))
        return grads, sums

    up_grad, up_sums = beside([down_sum], up_backward, mlp_grad)
    up_wgrad = [dot_tn(mlp_low, part).astype(jnp.bfloat16) for part in up_grad]
    up_sum = SumChain([up_wgrad])
    mlp_value = sum(dot_nt(hidden_low[h], down_whole[h]) for h in chunks)
    mlp_value = in_blocks(mlp_value + bias_all[3 * D + FF : 4 * D + FF])
    block_out = in_rows(residual_mid + gate_mlp * mlp_value)

    def mid_backward(parts):
        norm_grad = in_blocks(sum(dot_nt(parts[h], up_whole[h]) for h in chunks))
        grad = cotangent + norm_back(norm_mlp, inverse_mlp, norm_grad * (1.0 + scale_mlp))
        low = in_rows((grad * gate_attn).astype(jnp.bfloat16))
        return low, grad, norm_grad, jnp.sum(low.astype(jnp.float32), axis=0)

    attn_grad, mid_grad, mlp_norm_grad, attn_grad_sum = beside(
        [down_sum, up_sum], mid_backward, up_grad
    )
    early = jnp.concatenate(
        [attn_grad_sum]
        + up_sums
        + [
            jnp.sum(mlp_grad.astype(jnp.float32), axis=0),
            latent_sums(mid_grad * attn_value).reshape(-1),
            latent_sums(mlp_norm_grad).reshape(-1),
            latent_sums(mlp_norm_grad * norm_mlp).reshape(-1),
            latent_sums(cotangent * mlp_value).reshape(-1),
        ]
    )
    heads_grad = [dot_nn(attn_grad, part).astype(jnp.bfloat16) for part in out_whole]
    early, heads_grad = lax.optimization_barrier((early, heads_grad))
    early_all = lax.all_gather(early.reshape(-1, LANES), both, axis=0, tiled=False)
    out_wgrad = jnp.stack([dot_tn(attn_grad, part) for part in head_low])
    out_summed = lax.psum_scatter(
        out_wgrad.reshape(device_count, D // dp_count, width),
        ("tensor", "dp"),
        scatter_dimension=0,
        tiled=False,
    ).T

    qkv_grad = []
    for h in chunks:
        qkv_grad.append(
            beside(
                [down_sum, up_sum],
                lambda grad: attend_backward(
                    qkv_ext[h], head_low[h], grad, log_totals[h], starts, block_rows, block_count
                ),
                heads_grad[h],
            )
        )
    early_all, qkv_grad = lax.optimization_barrier((early_all, qkv_grad))
    early_all = early_all.reshape(device_count, -1)
    norm_grad_ext, norm_ext = beside(
        [down_sum, up_sum],
        lambda parts: (sum(dot_nt(parts[0][h], qkv_whole[h]) for h in chunks), parts[1]),
        (qkv_grad, norm_ext),
    )

    qkv_sums = [jnp.sum(part.astype(jnp.float32), axis=0) for part in qkv_grad]
    by_latent = norm_grad_ext.reshape(window, L, D)
    late = jnp.concatenate(
        [part[:width] for part in qkv_sums]
        + [part[2 * width :] for part in qkv_sums]
        + [
            jnp.sum(by_latent, axis=1).reshape(-1),
            jnp.sum(by_latent * norm_ext.astype(jnp.float32), axis=1).reshape(-1),
        ]
    )
    late_sums = GatherChain(late.reshape(-1, LANES))
    norm_grad_ext = norm_grad_ext.reshape(-1, block_rows, D)
    sent = [
        lax.dynamic_slice_in_dim(norm_grad_ext, target, size // block_rows, 0).astype(jnp.bfloat16)
        for (size, pieces), (source, target) in zip(rounds, places)
    ]
    qkv_grad, sent = lax.optimization_barrier((qkv_grad, sent))
    returned = Received(
        [
            lax.ppermute(part, both, [(piece[1], piece[0]) for piece in pieces])
            for part, (size, pieces) in zip(sent, rounds)
        ]
    )
    qkv_wgrad = beside(
        [late_sums, down_sum, up_sum],
        lambda parts: [dot_tn(attn_ext, part).astype(jnp.bfloat16) for part in parts],
        qkv_grad,
    )
    qkv_sum = SumChain([qkv_wgrad])
    chains = [qkv_sum, late_sums, down_sum, up_sum]
    advance(chains + [returned])
    attn_norm_grad = lax.dynamic_slice_in_dim(norm_grad_ext, start_block, block_count, 0)
    for (size, pieces), (source, target), got in zip(rounds, places, returned.got):
        old = lax.dynamic_slice_in_dim(attn_norm_grad, source, size // block_rows, 0)
        attn_norm_grad = lax.dynamic_update_slice_in_dim(
            attn_norm_grad, old + got.astype(jnp.float32), source, 0
        )
    tokens_grad = in_rows(
        mid_grad + norm_back(norm_attn, inverse_attn, attn_norm_grad * (1.0 + scale_attn))
    )
    while not all(chain.done() for chain in chains):
        advance(chains)
    late_all, order = late_sums.values.reshape(device_count, -1), late_sums.order

    spread = np.zeros((latent_count, device_count, window), np.float32)
    for i, first in enumerate(first_latents):
        for w in range(window):
            if first + w < latent_count:
                spread[first + w, i, w] = 1.0

    def latent_totals(gathered, devices):
        terms = gathered.reshape(device_count * window, D)
        picks = jnp.asarray(spread[:, devices].reshape(latent_count, -1))
        return jnp.dot(picks, terms, precision=highest, preferred_element_type=jnp.float32)

    early_bias = 2 * D + FF
    step = window * D
    mod_grads = [
        latent_totals(late_all[:, 2 * D + i * step : 2 * D + (i + 1) * step], order)
        for i in range(2)
    ] + [
        latent_totals(
            early_all[:, early_bias + i * step : early_bias + (i + 1) * step],
            np.arange(device_count),
        )
        for i in range(4)
    ]
    mod_grad = jnp.concatenate(mod_grads, axis=1)
    bias_grad = jnp.concatenate(
        [
            jnp.sum(late_all[:, : 2 * D], axis=0),
            jnp.sum(early_all[:, :early_bias], axis=0),
            jnp.sum(mod_grad, axis=0),
        ]
    )
    ada_wgrad = jnp.dot(
        silu_low.astype(jnp.float32).T,
        mod_grad,
        precision=highest,
        preferred_element_type=jnp.float32,
    )
    cond_inner = jnp.dot(
        mod_grad,
        ada_low.astype(jnp.float32).T,
        precision=highest,
        preferred_element_type=jnp.float32,
    )
    unused, silu_pull = jax.vjp(jax.nn.silu, cond_value)
    condition_grad = silu_pull(cond_inner)[0]
    qkv_summed = qkv_sum.result[0].reshape(qkv_weight.shape)
    up_summed = up_sum.result[0]
    down_summed = down_sum.result[0].T
    qkv_new = adam_update(qkv_weight, qkv_summed, qkv_first, qkv_second, 3.0 / math.sqrt(D))
    out_new = adam_update(out_weight, out_summed, out_first, out_second, 3.0 / math.sqrt(D // 4))
    up_new = adam_update(up_weight, up_summed, up_first, up_second, 3.0 / math.sqrt(D))
    down_new = adam_update(down_weight, down_summed, down_first, down_second, 3.0 / math.sqrt(FF))
    ada_new = adam_update(ada_weight, ada_wgrad, ada_first, ada_second, 3.0 / math.sqrt(D))
    bias_new = adam_update(bias_all, bias_grad, bias_first, bias_second, 0.9)
    return (
        block_out,
        tokens_grad,
        condition_grad,
        *qkv_new,
        *out_new,
        *up_new,
        *down_new,
        *ada_new,
        *bias_new,
    )


def solution(mesh):
    weights = (
        P("dp", None, "tensor"),
        P("tensor", "dp"),
        P("dp", "tensor"),
        P("tensor", "dp"),
        P("dp", None),
        P(),
    )
    tokens = P(both, None)
    return jax.shard_map(
        on_device,
        mesh=mesh,
        in_specs=(tokens, P(None, "dp"), tokens, *weights, *weights, *weights),
        out_specs=(tokens, tokens, P(None, "dp"))
        + tuple(spec for spec in weights for unused in range(3)),
        check_vma=False,
    )
```

```python
import math

import jax
import jax.numpy as jnp
import numpy as np
from jax import lax
from jax.experimental import pallas as pl
from jax.experimental.pallas import tpu as pltpu
from jax.sharding import PartitionSpec as P

D = 1024
HD = 64
FF = 4096
L = 1024
STEP = 10
LANES = 128
VMEM_BYTES = 48 * 1024 * 1024


eps_norm = 1e-06
beta_one = 0.9
beta_two = 0.95
adam_eps = 1e-08
decay_rate = 0.01
highest = lax.Precision.HIGHEST
both = ("dp", "tensor")


def halo_plan(device_count, row_count):
    by_size = {}
    for dst in range(device_count):
        low = dst * row_count // L * L
        high = -(-(dst + 1) * row_count // L) * L
        for src in range(low // row_count, -(-high // row_count)):
            start = max(low, src * row_count)
            stop = min(high, (src + 1) * row_count)
            if src != dst and start < stop:
                piece = (src, dst, start - src * row_count, start - low)
                by_size.setdefault(stop - start, []).append(piece)
    rounds = []
    for size in sorted(by_size, reverse=True):
        left = by_size[size]
        while left:
            taken, later, sources, targets = [], [], set(), set()
            for piece in left:
                if piece[0] in sources or piece[1] in targets:
                    later.append(piece)
                else:
                    taken.append(piece)
                    sources.add(piece[0])
                    targets.add(piece[1])
            rounds.append((size, taken))
            left = later
    return rounds


def window_latents(device_count, row_count):
    widths = [
        -(-(i + 1) * row_count // L) - i * row_count // L for i in range(device_count)
    ]
    return max(widths)


def look_up(table, index):
    return lax.dynamic_index_in_dim(jnp.asarray(np.array(table, np.int32)), index, 0, False)


def norm_parts(values):
    center = values - jnp.mean(values, axis=-1, keepdims=True)
    spread = jnp.mean(center * center, axis=-1, keepdims=True)
    inverse = lax.rsqrt(spread + eps_norm)
    return (center * inverse, inverse)


def norm_back(normed, inverse, cotangent):
    mean_grad = jnp.mean(cotangent, axis=-1, keepdims=True)
    mean_dot = jnp.mean(cotangent * normed, axis=-1, keepdims=True)
    return inverse * (cotangent - mean_grad - normed * mean_dot)


def gelu_tanh(values):
    return jax.nn.gelu(values, approximate=True)


def adam_update(weight, gradient, first_old, second, step_rate):
    first_new = beta_one * first_old + (1.0 - beta_one) * gradient
    second_new = beta_two * second + (1.0 - beta_two) * gradient * gradient
    first_hat = first_new / (1.0 - beta_one**STEP)
    second_hat = second_new / (1.0 - beta_two**STEP)
    weight_new = weight - step_rate * (
        first_hat / (jnp.sqrt(second_hat) + adam_eps) + decay_rate * weight
    )
    return (first_new, second_new, weight_new)


def dot_nt(left, right):
    return lax.dot_general(
        left, right, (((1,), (1,)), ((), ())), preferred_element_type=jnp.float32
    )


def dot_nn(left, right):
    return lax.dot_general(
        left, right, (((1,), (0,)), ((), ())), preferred_element_type=jnp.float32
    )


def dot_tn(left, right):
    return lax.dot_general(
        left, right, (((0,), (0,)), ((), ())), preferred_element_type=jnp.float32
    )


def head_masks():
    lane = lax.broadcasted_iota(jnp.int32, (1, LANES), 1)
    low_half = (lane < HD).astype(jnp.bfloat16)
    return (low_half, (lane >= HD).astype(jnp.bfloat16))


def forward_kernel(start_ref, query_ref, key_ref, value_ref, heads_ref, log_ref):
    masks = head_masks()
    pairs = query_ref.shape[1] // LANES
    group = 2 if pairs % 2 == 0 else 1

    @pl.loop(0, pairs // group)
    def group_step(step):
        scores, turned = [], []
        for i in range(group):
            cols = pl.ds(pl.multiple_of((step * group + i) * LANES, LANES), LANES)
            query = query_ref[:, cols] * jnp.bfloat16(HD**-0.5)
            scores += [dot_nt(key_ref[:, cols], query * mask) for mask in masks]
            turned.append(value_ref[:, cols].T)
        for i in range(group):
            pair = step * group + i
            outs = []
            for half in range(2):
                score = scores[2 * i + half]
                row_max = jnp.max(score, axis=0, keepdims=True)
                weights = jnp.exp(score - row_max)
                row_sum = jnp.sum(weights, axis=0, keepdims=True)
                out = dot_nn(
                    turned[i][half * HD : (half + 1) * HD], weights.astype(jnp.bfloat16)
                )
                outs.append(out / row_sum)
                log_ref[0, pl.ds(2 * pair + half, 1), :] = row_max + jnp.log(row_sum)
            cols = pl.ds(pl.multiple_of(pair * LANES, LANES), LANES)
            heads_ref[:, cols] = jnp.concatenate(outs, axis=0).T.astype(jnp.bfloat16)


def backward_kernel(
    start_ref,
    query_ref,
    key_ref,
    value_ref,
    heads_ref,
    grad_ref,
    log_ref,
    out_ref,
    key_acc,
    value_acc,
):
    step = pl.program_id(0)
    block_rows, width = query_ref.shape
    block = start_ref[0] + step
    latent = block * block_rows // L
    own = pl.ds(pl.multiple_of(block * block_rows, block_rows), block_rows)
    masks = head_masks()
    key_rows = L // 2

    @pl.when(step == 0)
    def clear():
        key_acc[...] = jnp.zeros_like(key_acc)
        value_acc[...] = jnp.zeros_like(value_acc)
        out_ref[:, :width] = jnp.zeros((out_ref.shape[0], width), out_ref.dtype)

    @pl.loop(0, width // LANES)
    def pair_step(pair):
        cols = pl.ds(pl.multiple_of(pair * LANES, LANES), LANES)
        query = query_ref[:, cols] * jnp.bfloat16(HD**-0.5)
        grad = grad_ref[:, cols]
        dots = (grad.astype(jnp.float32) * heads_ref[:, cols].astype(jnp.float32)).T
        key_turned = key_ref[:, cols].T
        queries = [query * mask for mask in masks]
        grads = [grad * mask for mask in masks]
        logs = [log_ref[0, pl.ds(2 * pair + half, 1), :] for half in range(2)]
        row_dots = [
            jnp.sum(dots[half * HD : (half + 1) * HD], axis=0, keepdims=True) for half in range(2)
        ]
        joined = block_rows % LANES == 0
        if joined:
            queries, grads = (
                [jnp.concatenate(queries, axis=0)],
                [jnp.concatenate(grads, axis=0)],
            )
            logs, row_dots = (
                [jnp.concatenate(logs, axis=1)],
                [jnp.concatenate(row_dots, axis=1)],
            )
        query_grads = [0.0, 0.0]
        for start in range(0, L, key_rows):
            key = key_ref[start : start + key_rows, cols]
            value = value_ref[start : start + key_rows, cols]
            value_part = key_part = 0.0
            for i in range(len(queries)):
                prob = jnp.exp(dot_nt(key, queries[i]) - logs[i])
                prob_grad = dot_nt(value, grads[i])
                score_grad = (prob * (prob_grad - row_dots[i])).astype(jnp.bfloat16)
                value_part += dot_nn(prob.astype(jnp.bfloat16), grads[i])
                key_part += dot_nn(score_grad, queries[i])
                for half in range(2) if joined else (i,):
                    mine = score_grad
                    if joined:
                        mine = score_grad[:, half * block_rows : (half + 1) * block_rows]
                    turned = key_turned[half * HD : (half + 1) * HD, start : start + key_rows]
                    query_grads[half] += dot_nn(turned, mine)
            rows = pl.ds(pl.multiple_of(latent * L + start, key_rows), key_rows)
            value_acc[rows, cols] += value_part
            key_acc[rows, cols] += key_part
        turned = jnp.concatenate(query_grads, axis=0).T * HD**-0.5
        out_ref[own, cols] = turned.astype(jnp.bfloat16)

    @pl.when(step == pl.num_programs(0) - 1)
    def finish():
        out_ref[:, width : 2 * width] = key_acc[...].astype(jnp.bfloat16)
        out_ref[:, 2 * width :] = value_acc[...].astype(jnp.bfloat16)


def qkv_specs(block_rows, width):
    return [
        pl.BlockSpec((block_rows, width), lambda b, start: (start[0] + b, 0)),
        pl.BlockSpec((L, width), lambda b, start: ((start[0] + b) * block_rows // L, 1)),
        pl.BlockSpec((L, width), lambda b, start: ((start[0] + b) * block_rows // L, 2)),
    ]


def attend_forward(qkv_ext, start_block, block_rows, block_count):
    width = qkv_ext.shape[1] // 3
    heads = width // HD
    cost = 4 * block_rows * block_count * L * width
    return pl.pallas_call(
        forward_kernel,
        grid_spec=pltpu.PrefetchScalarGridSpec(
            num_scalar_prefetch=1,
            grid=(block_count,),
            in_specs=qkv_specs(block_rows, width),
            out_specs=[
                pl.BlockSpec((block_rows, width), lambda b, start: (b, 0)),
                pl.BlockSpec((1, heads, block_rows), lambda b, start: (b, 0, 0)),
            ],
        ),
        out_shape=[
            jax.ShapeDtypeStruct((block_rows * block_count, width), jnp.bfloat16),
            jax.ShapeDtypeStruct((block_count, heads, block_rows), jnp.float32),
        ],
        compiler_params=pltpu.CompilerParams(vmem_limit_bytes=VMEM_BYTES),
        cost_estimate=pl.CostEstimate(
            flops=4 * cost, bytes_accessed=qkv_ext.size * 4, transcendentals=cost // 4 // HD
        ),
        name="attend_forward",
    )(start_block, qkv_ext, qkv_ext, qkv_ext)


def attend_backward(
    qkv_ext, heads_low, heads_grad, log_totals, start_block, block_rows, block_count
):
    ext_rows, width = qkv_ext.shape[0], qkv_ext.shape[1] // 3
    heads = width // HD
    cost = 10 * block_rows * block_count * L * width
    return pl.pallas_call(
        backward_kernel,
        grid_spec=pltpu.PrefetchScalarGridSpec(
            num_scalar_prefetch=1,
            grid=(block_count,),
            in_specs=qkv_specs(block_rows, width)
            + [
                pl.BlockSpec((block_rows, width), lambda b, start: (b, 0)),
                pl.BlockSpec((block_rows, width), lambda b, start: (b, 0)),
                pl.BlockSpec((1, heads, block_rows), lambda b, start: (b, 0, 0)),
            ],
            out_specs=pl.BlockSpec((ext_rows, 3 * width), lambda b, start: (0, 0)),
            scratch_shapes=[
                pltpu.VMEM((ext_rows, width), jnp.float32),
                pltpu.VMEM((ext_rows, width), jnp.float32),
            ],
        ),
        out_shape=jax.ShapeDtypeStruct((ext_rows, 3 * width), jnp.bfloat16),
        compiler_params=pltpu.CompilerParams(vmem_limit_bytes=VMEM_BYTES),
        cost_estimate=pl.CostEstimate(
            flops=4 * cost, bytes_accessed=qkv_ext.size * 6, transcendentals=cost // 10 // HD
        ),
        name="attend_backward",
    )(start_block, qkv_ext, qkv_ext, qkv_ext, heads_low, heads_grad, log_totals)


def axis_bits():
    dp_bits = lax.axis_size("dp").bit_length() - 1
    tensor_bits = lax.axis_size("tensor").bit_length() - 1
    z_bits = [("dp", bit) for bit in (dp_bits - 1, dp_bits - 2)]
    x_bits = [("dp", bit) for bit in range(dp_bits - 3, 0, -1)]
    y_bits = [("tensor", bit) for bit in range(tensor_bits - 1, -1, -1)]
    return z_bits, x_bits, y_bits


def own_bit(place):
    return lax.axis_index(place[0]) >> place[1] & 1


def swap(values, place):
    axis, bit = place
    route = [(i, i ^ 1 << bit) for i in range(lax.axis_size(axis))]
    return lax.ppermute(values, axis, route)


def add_low(kept, got):
    return (kept.astype(jnp.float32) + got.astype(jnp.float32)).astype(jnp.bfloat16)


def pick_half(values, axis, bit):
    return lax.dynamic_index_in_dim(values, bit, axis, False)


class SumChain:
    def __init__(self, groups):
        dp_count = lax.axis_size("dp")
        rows, columns = D // dp_count, groups[0][0].shape[1]
        z_bits, x_bits, y_bits = axis_bits()
        parts = [part.reshape(dp_count // 2, 2, rows, columns) for group in groups for part in group]
        places = ["group"] + y_bits + z_bits + x_bits
        self.shape = (len(groups),) + (2,) * (len(places) - 1) + (rows, columns)
        self.parts = parts
        self.places = places
        self.stages = [[("dp", 0)]]
        self.stages += [list(both) for both in zip(x_bits + y_bits, y_bits + x_bits)]
        self.stages += [[z_bits[0]], [z_bits[1]]]
        self.z_bits = z_bits
        self.stage = 0

    def done(self):
        return self.stage == len(self.stages)

    def sends(self):
        stage = self.stages[self.stage]
        if self.stage == 0:
            bit = own_bit(stage[0])
            self.kept = [pick_half(part, 1, bit) for part in self.parts]
            return [pick_half(part, 1, 1 - bit) for part in self.parts]
        if self.stage == len(self.stages) - 2:
            upper = own_bit(stage[0]) == 1
            first, second = self.halves
            self.kept = [jnp.where(upper, second, first)]
            return [jnp.where(upper, first, second)]
        sent, self.kept = [], []
        for i, place in enumerate(stage):
            axis, bit = self.labels[i].index(place), own_bit(place)
            sent.append(pick_half(self.halves[i], axis, 1 - bit))
            self.kept.append(pick_half(self.halves[i], axis, bit))
            self.labels[i] = [label for label in self.labels[i] if label != place]
        return sent

    def swap(self, sent):
        places = self.stages[self.stage]
        if self.stage == 0:
            places = places * len(sent)
        return [swap(values, place) for values, place in zip(sent, places)]

    def receive(self, got):
        self.stage += 1
        if self.stage == 1:
            self.kept, got = [jnp.stack(self.kept)], [jnp.stack(got)]
        if self.done():
            self.result = self.kept[0].astype(jnp.float32) + got[0].astype(jnp.float32)
            return
        totals = [add_low(kept, part) for kept, part in zip(self.kept, got)]
        if self.stage == 1:
            total = totals[0].reshape(self.shape)
            high = self.places.index(self.z_bits[0])
            rest = [place for place in self.places if place != self.z_bits[0]]
            totals = [lax.index_in_dim(total, i, high, False) for i in range(2)]
            self.labels = [rest, rest]
        elif self.stage == len(self.stages) - 1:
            self.labels = [["group", self.z_bits[1]]]
        self.halves = totals


class GatherChain:
    def __init__(self, values):
        z_bits, x_bits, y_bits = axis_bits()
        self.values, self.order = values[None], np.zeros((1,), np.int64)
        self.stages = z_bits + x_bits + y_bits + [("dp", 0)]
        self.stage = 0

    def done(self):
        return self.stage == len(self.stages)

    def sends(self):
        return [self.values]

    def swap(self, sent):
        return [swap(sent[0], self.stages[self.stage])]

    def receive(self, got):
        place = self.stages[self.stage]
        upper = own_bit(place) == 1
        self.values = jnp.concatenate(
            [jnp.where(upper, got[0], self.values), jnp.where(upper, self.values, got[0])]
        )
        weight = (lax.axis_size("tensor") if place[0] == "dp" else 1) << place[1]
        self.order = np.concatenate([self.order, self.order + weight])
        self.stage += 1


class Received:
    def __init__(self, values):
        self.values, self.got = values, None

    def done(self):
        return self.got is not None

    def sends(self):
        return self.values

    def swap(self, sent):
        return sent

    def receive(self, got):
        self.got = got


def advance(chains):
    chains = [chain for chain in chains if not chain.done()]
    got = lax.optimization_barrier([chain.swap(chain.sends()) for chain in chains])
    for chain, values in zip(chains, got):
        chain.receive(values)


def beside(chains, work, operand):
    chains = [chain for chain in chains if not chain.done()]
    operand, sent = lax.optimization_barrier((operand, [chain.sends() for chain in chains]))
    got = [chain.swap(values) for chain, values in zip(chains, sent)]
    result, got = lax.optimization_barrier((work(operand), got))
    for chain, values in zip(chains, got):
        chain.receive(values)
    return result


def gather_rows(shard):
    whole = lax.all_gather(shard, ("tensor", "dp"), axis=0, tiled=True)
    tensor_count = lax.axis_size("tensor")
    return whole.reshape(tensor_count, D, shard.shape[1])


def on_device(
    tokens_in,
    condition,
    out_grad,
    qkv_weight,
    out_weight,
    up_weight,
    down_weight,
    ada_weight,
    bias_all,
    qkv_first,
    out_first,
    up_first,
    down_first,
    ada_first,
    bias_first,
    qkv_second,
    out_second,
    up_second,
    down_second,
    ada_second,
    bias_second,
):
    tensor_count = lax.axis_size("tensor")
    dp_count = lax.axis_size("dp")
    device_count = dp_count * tensor_count
    dp_index = lax.axis_index("dp")
    device = dp_index * tensor_count + lax.axis_index("tensor")
    row_count = tokens_in.shape[0]
    latent_count = condition.shape[0]
    width = D // tensor_count
    block_rows = math.gcd(row_count, L)
    block_count = row_count // block_rows
    rounds = halo_plan(device_count, row_count)
    window = window_latents(device_count, row_count)
    dp_window = window_latents(dp_count, row_count * tensor_count)
    first_latents = [i * row_count // L for i in range(device_count)]
    dp_latents = [i * row_count * tensor_count // L for i in range(dp_count)]
    first_latent = look_up(first_latents, device)
    start_block = look_up(
        [i * row_count % L // block_rows for i in range(device_count)], device
    )

    hidden = FF // tensor_count
    chunks = range(tensor_count)
    attn_shard = jnp.concatenate(
        [
            qkv_weight.astype(jnp.bfloat16).reshape(-1, 3 * width),
            out_weight.astype(jnp.bfloat16).T,
        ],
        axis=1,
    )
    attn_whole = gather_rows(attn_shard)
    qkv_whole = [attn_whole[h, :, : 3 * width] for h in chunks]
    out_whole = [attn_whole[h, :, 3 * width :] for h in chunks]
    mlp_shard = jnp.concatenate(
        [up_weight.astype(jnp.bfloat16), down_weight.astype(jnp.bfloat16).T], axis=1
    )
    mlp_whole = gather_rows(mlp_shard)
    up_whole = [mlp_whole[h, :, :hidden] for h in chunks]
    down_whole = [mlp_whole[h, :, hidden:] for h in chunks]

    cond_value = condition.astype(jnp.float32)
    silu_low = jax.nn.silu(cond_value).astype(jnp.bfloat16)
    ada_low = ada_weight.astype(jnp.bfloat16)
    picked = [min(first, latent_count - dp_window) for first in dp_latents]
    silu_picked = jnp.concatenate([silu_low[first : first + dp_window] for first in picked])
    ada_part = dot_nn(silu_picked, ada_low).reshape(dp_count, dp_window, 6 * D)

    def in_blocks(values):
        return values.reshape(block_count, block_rows, -1)

    def in_rows(values):
        return values.reshape(row_count, -1)

    tokens = in_blocks(tokens_in)
    cotangent = in_blocks(out_grad)
    norm_attn, inverse_attn = norm_parts(tokens)
    ada_part, norm_low = lax.optimization_barrier((ada_part, norm_attn.astype(jnp.bfloat16)))
    norm_ext = jnp.zeros((window * L // block_rows, block_rows, D), jnp.bfloat16)
    places = []
    for size, pieces in rounds:
        source = [0] * device_count
        target = [i * row_count % L // block_rows for i in range(device_count)]
        for src, dst, src_row, dst_row in pieces:
            source[src] = src_row // block_rows
            target[dst] = dst_row // block_rows
        places.append((look_up(source, device), look_up(target, device)))
    for (size, pieces), (source, target) in zip(rounds, places):
        sent = lax.dynamic_slice_in_dim(norm_low, source, size // block_rows, 0)
        got = lax.ppermute(sent, both, [(piece[0], piece[1]) for piece in pieces])
        norm_ext = lax.dynamic_update_slice_in_dim(norm_ext, got, target, 0)
    norm_ext = lax.dynamic_update_slice_in_dim(norm_ext, norm_low, start_block, 0)

    ada_parts = lax.all_to_all(ada_part, "dp", split_axis=0, concat_axis=0, tiled=True)
    mod_dp = jnp.sum(ada_parts, axis=0) + bias_all[4 * D + FF :]
    mod_dp = jnp.concatenate([mod_dp, jnp.zeros((window, 6 * D), jnp.float32)])
    mod_window = lax.dynamic_slice_in_dim(
        mod_dp, first_latent - look_up(picked, dp_index), window, 0
    )
    block_latent = (start_block + jnp.arange(block_count, dtype=jnp.int32)) * block_rows // L
    latent_pick = (
        block_latent[None, :] == jnp.arange(window, dtype=jnp.int32)[:, None]
    ).astype(jnp.float32)
    mod_blocks = jnp.sum(latent_pick[:, :, None] * mod_window[:, None, :], axis=0)
    mod_blocks = mod_blocks.reshape(block_count, 1, 6 * D)
    shift_attn, scale_attn, gate_attn, shift_mlp, scale_mlp, gate_mlp = (
        mod_blocks[:, :, i * D : (i + 1) * D] for i in range(6)
    )

    def latent_sums(values):
        return jnp.sum(latent_pick[:, :, None] * jnp.sum(values, axis=1)[None], axis=1)

    norm_ext = norm_ext.reshape(window, L, D)
    attn_ext = (
        norm_ext.astype(jnp.float32) * (1.0 + mod_window[:, None, D : 2 * D])
        + mod_window[:, None, :D]
    ).astype(jnp.bfloat16)
    attn_own = (norm_attn * (1.0 + scale_attn) + shift_attn).astype(jnp.bfloat16)
    attn_ext = lax.dynamic_update_slice_in_dim(
        attn_ext.reshape(-1, block_rows, D), attn_own, start_block, 0
    ).reshape(window * L, D)

    starts = start_block.reshape(1)
    qkv_ext, head_low, log_totals = [], [], []
    for h in chunks:
        own = slice(h * width, (h + 1) * width)
        bias = jnp.concatenate(
            [bias_all[:D][own], jnp.zeros((width,), jnp.float32), bias_all[D : 2 * D][own]]
        )
        qkv_ext.append((dot_nn(attn_ext, qkv_whole[h]) + bias).astype(jnp.bfloat16))
        heads, logs = attend_forward(qkv_ext[h], starts, block_rows, block_count)
        head_low.append(heads)
        log_totals.append(logs)
    attn_value = sum(dot_nt(head_low[h], out_whole[h]) for h in chunks)
    attn_value = in_blocks(attn_value + bias_all[2 * D : 3 * D])
    residual_mid = tokens + gate_attn * attn_value
    norm_mlp, inverse_mlp = norm_parts(residual_mid)
    mlp_low = in_rows((norm_mlp * (1.0 + scale_mlp) + shift_mlp).astype(jnp.bfloat16))
    mlp_grad = in_rows((cotangent * gate_mlp).astype(jnp.bfloat16))

    up_values = [
        dot_nn(mlp_low, up_whole[h]) + bias_all[3 * D + h * hidden : 3 * D + (h + 1) * hidden]
        for h in chunks
    ]
    hidden_low = [gelu_tanh(up_value).astype(jnp.bfloat16) for up_value in up_values]
    down_sum = SumChain([[dot_tn(mlp_grad, part).astype(jnp.bfloat16) for part in hidden_low]])

    def up_backward(grad):
        grads, sums = [], []
        for h in chunks:
            unused, gelu_pull = jax.vjp(gelu_tanh, up_values[h])
            part = gelu_pull(dot_nn(grad, down_whole[h]))[0].astype(jnp.bfloat16)
            grads.append(part)
            sums.append(jnp.sum(part.astype(jnp.float32), axis=0))
        return grads, sums

    up_grad, up_sums = beside([down_sum], up_backward, mlp_grad)
    up_wgrad = [dot_tn(mlp_low, part).astype(jnp.bfloat16) for part in up_grad]
    up_sum = SumChain([up_wgrad])
    mlp_value = sum(dot_nt(hidden_low[h], down_whole[h]) for h in chunks)
    mlp_value = in_blocks(mlp_value + bias_all[3 * D + FF : 4 * D + FF])
    block_out = in_rows(residual_mid + gate_mlp * mlp_value)

    def mid_backward(parts):
        norm_grad = in_blocks(sum(dot_nt(parts[h], up_whole[h]) for h in chunks))
        grad = cotangent + norm_back(norm_mlp, inverse_mlp, norm_grad * (1.0 + scale_mlp))
        low = in_rows((grad * gate_attn).astype(jnp.bfloat16))
        return low, grad, norm_grad, jnp.sum(low.astype(jnp.float32), axis=0)

    attn_grad, mid_grad, mlp_norm_grad, attn_grad_sum = beside(
        [down_sum, up_sum], mid_backward, up_grad
    )
    early = jnp.concatenate(
        [attn_grad_sum]
        + up_sums
        + [
            jnp.sum(mlp_grad.astype(jnp.float32), axis=0),
            latent_sums(mid_grad * attn_value).reshape(-1),
            latent_sums(mlp_norm_grad).reshape(-1),
            latent_sums(mlp_norm_grad * norm_mlp).reshape(-1),
            latent_sums(cotangent * mlp_value).reshape(-1),
        ]
    )
    heads_grad = [dot_nn(attn_grad, part).astype(jnp.bfloat16) for part in out_whole]
    early, heads_grad = lax.optimization_barrier((early, heads_grad))
    early_all = lax.all_gather(early.reshape(-1, LANES), both, axis=0, tiled=False)
    out_wgrad = jnp.stack([dot_tn(attn_grad, part) for part in head_low])
    out_summed = lax.psum_scatter(
        out_wgrad.reshape(device_count, D // dp_count, width),
        ("tensor", "dp"),
        scatter_dimension=0,
        tiled=False,
    ).T

    qkv_grad = []
    for h in chunks:
        qkv_grad.append(
            beside(
                [down_sum, up_sum],
                lambda grad: attend_backward(
                    qkv_ext[h], head_low[h], grad, log_totals[h], starts, block_rows, block_count
                ),
                heads_grad[h],
            )
        )
    early_all = Received([early_all])
    norm_grad_ext, norm_ext = beside(
        [down_sum, up_sum],
        lambda parts: (sum(dot_nt(parts[0][h], qkv_whole[h]) for h in chunks), parts[1]),
        (qkv_grad, norm_ext),
    )

    qkv_sums = [jnp.sum(part.astype(jnp.float32), axis=0) for part in qkv_grad]
    by_latent = norm_grad_ext.reshape(window, L, D)
    late = jnp.concatenate(
        [part[:width] for part in qkv_sums]
        + [part[2 * width :] for part in qkv_sums]
        + [
            jnp.sum(by_latent, axis=1).reshape(-1),
            jnp.sum(by_latent * norm_ext.astype(jnp.float32), axis=1).reshape(-1),
        ]
    )
    late_sums = GatherChain(late.reshape(-1, LANES))
    norm_grad_ext = norm_grad_ext.reshape(-1, block_rows, D)
    sent = [
        lax.dynamic_slice_in_dim(norm_grad_ext, target, size // block_rows, 0).astype(jnp.bfloat16)
        for (size, pieces), (source, target) in zip(rounds, places)
    ]
    qkv_grad, sent = lax.optimization_barrier((qkv_grad, sent))
    got = [
        lax.ppermute(part, both, [(piece[1], piece[0]) for piece in pieces])
        for part, (size, pieces) in zip(sent, rounds)
    ]
    large_rounds = len(rounds) * 2 // 3
    later_got, first_got = Received(got[:large_rounds]), got[large_rounds:]

    def qkv_backward(parts):
        return [dot_tn(attn_ext, part).astype(jnp.bfloat16) for part in parts]

    half = (tensor_count + 1) // 2
    first_wgrad = beside([late_sums], qkv_backward, qkv_grad[:half])
    first_wgrad, first_got, rest = lax.optimization_barrier(
        (first_wgrad, first_got, qkv_grad[half:])
    )
    qkv_wgrad = first_wgrad + beside([late_sums, down_sum, up_sum], qkv_backward, rest)
    qkv_sum = SumChain([qkv_wgrad])
    chains = [qkv_sum, late_sums, down_sum, up_sum]
    advance(chains + [later_got])
    advance(chains + [early_all])
    early_all = early_all.got[0].reshape(device_count, -1)
    attn_norm_grad = lax.dynamic_slice_in_dim(norm_grad_ext, start_block, block_count, 0)
    for (size, pieces), (source, target), got in zip(
        rounds, places, list(later_got.got) + list(first_got)
    ):
        old = lax.dynamic_slice_in_dim(attn_norm_grad, source, size // block_rows, 0)
        attn_norm_grad = lax.dynamic_update_slice_in_dim(
            attn_norm_grad, old + got.astype(jnp.float32), source, 0
        )
    tokens_grad = in_rows(
        mid_grad + norm_back(norm_attn, inverse_attn, attn_norm_grad * (1.0 + scale_attn))
    )
    while not all(chain.done() for chain in chains):
        advance(chains)
    late_all, order = late_sums.values.reshape(device_count, -1), late_sums.order

    spread = np.zeros((latent_count, device_count, window), np.float32)
    for i, first in enumerate(first_latents):
        for w in range(window):
            if first + w < latent_count:
                spread[first + w, i, w] = 1.0

    def latent_totals(gathered, devices):
        terms = gathered.reshape(device_count * window, D)
        picks = jnp.asarray(spread[:, devices].reshape(latent_count, -1))
        return jnp.dot(picks, terms, precision=highest, preferred_element_type=jnp.float32)

    early_bias = 2 * D + FF
    step = window * D
    mod_grads = [
        latent_totals(late_all[:, 2 * D + i * step : 2 * D + (i + 1) * step], order)
        for i in range(2)
    ] + [
        latent_totals(
            early_all[:, early_bias + i * step : early_bias + (i + 1) * step],
            np.arange(device_count),
        )
        for i in range(4)
    ]
    mod_grad = jnp.concatenate(mod_grads, axis=1)
    bias_grad = jnp.concatenate(
        [
            jnp.sum(late_all[:, : 2 * D], axis=0),
            jnp.sum(early_all[:, :early_bias], axis=0),
            jnp.sum(mod_grad, axis=0),
        ]
    )
    ada_wgrad = jnp.dot(
        silu_low.astype(jnp.float32).T,
        mod_grad,
        precision=highest,
        preferred_element_type=jnp.float32,
    )
    cond_inner = jnp.dot(
        mod_grad,
        ada_low.astype(jnp.float32).T,
        precision=highest,
        preferred_element_type=jnp.float32,
    )
    unused, silu_pull = jax.vjp(jax.nn.silu, cond_value)
    condition_grad = silu_pull(cond_inner)[0]
    qkv_summed = qkv_sum.result[0].reshape(qkv_weight.shape)
    up_summed = up_sum.result[0]
    down_summed = down_sum.result[0].T
    qkv_new = adam_update(qkv_weight, qkv_summed, qkv_first, qkv_second, 3.0 / math.sqrt(D))
    out_new = adam_update(out_weight, out_summed, out_first, out_second, 3.0 / math.sqrt(D // 4))
    up_new = adam_update(up_weight, up_summed, up_first, up_second, 3.0 / math.sqrt(D))
    down_new = adam_update(down_weight, down_summed, down_first, down_second, 3.0 / math.sqrt(FF))
    ada_new = adam_update(ada_weight, ada_wgrad, ada_first, ada_second, 3.0 / math.sqrt(D))
    bias_new = adam_update(bias_all, bias_grad, bias_first, bias_second, 0.9)
    return (
        block_out,
        tokens_grad,
        condition_grad,
        *qkv_new,
        *out_new,
        *up_new,
        *down_new,
        *ada_new,
        *bias_new,
    )


def solution(mesh):
    weights = (
        P("dp", None, "tensor"),
        P("tensor", "dp"),
        P("dp", "tensor"),
        P("tensor", "dp"),
        P("dp", None),
        P(),
    )
    tokens = P(both, None)
    return jax.shard_map(
        on_device,
        mesh=mesh,
        in_specs=(tokens, P(None, "dp"), tokens, *weights, *weights, *weights),
        out_specs=(tokens, tokens, P(None, "dp"))
        + tuple(spec for spec in weights for unused in range(3)),
        check_vma=False,
    )
```
